256 devices in a mesh: sector: 16 (over y_hi, z), radial: 16 (over x, y_lo, core).
Axes of the slice: x: 4, y: 4 (y_hi: 2, y_lo: 2; y = y_hi * 2 + y_lo), z: 8, core: 2. Of those that a mesh axis runs over, the one named last changes fastest.
Arguments:
- density: float32 [2048, 256, 128], P('sector', 'radial'), may hold values from 0.4 to 1.2
- swirl: float32 [2048, 256, 128], P('sector', 'radial'), may hold values from -4 to 4
- heat_rate: float32 [2048, 256, 128], P('sector', 'radial'), may hold values from 0.1 to 3
- acoustic: float32 [3, 2048, 128], P(None, 'sector'), may hold values from -5 to 5
- mode_impedance: float32 [1025], replicated, may hold values from 0.05 to 8
- mouth_azimuth: int32 [16], replicated, may hold values from 0 to 120, as said below
- mouth_radius: int32 [16], replicated, may hold values from 0 to 248, as said below
Outputs:
- density_next: float32 [2048, 256, 128], P('sector', 'radial')
- pressure: float32 [2048, 256, 128], P('sector', 'radial')
- acoustic_next: float32 [3, 2048, 128], P(None, 'sector')
The draws below stay inside these ranges and needn't reach their ends.
Inputs may be any that keep to these rules, and one draw needn't show every extreme that they name: Burner b's mouth starts at azimuthal cell b * 128 + mouth_azimuth[b] and spans 8 cells. Burner b's mouth spans radial cells mouth_radius[b] to mouth_radius[b] + 7.
All inputs are finite; a program needn't handle non-finite values.
Results may differ from the reference program's by a relative error of at most 0.00018.
Values sent between devices are 32-bit elements; how exact they have to be, the bound alone decides.
A program may use at most 128 MiB of HBM per device.

```python
import math
import jax
import jax.numpy as jnp

NZ = 128
BURNERS = 16
MOUTH = 8
SWEEPS = 4
SUBSTEPS = 8
NT = 2048
NR = 256


def draw_mouth_azimuth(key, part):
    top = NT // BURNERS - MOUTH
    values = jax.random.randint(jax.random.fold_in(key, 11), (BURNERS,), 0, top + 1)
    chosen = jax.random.randint(jax.random.fold_in(key, 12), (), 0, BURNERS)
    values = values.at[chosen].set(top)
    values = values.at[(chosen + 1) % BURNERS].set(0)
    return values.astype(jnp.int32)


def draw_mouth_radius(key, part):
    top = NR - MOUTH
    values = jax.random.randint(jax.random.fold_in(key, 21), (BURNERS,), 0, top + 1)
    chosen = jax.random.randint(jax.random.fold_in(key, 22), (), 0, BURNERS)
    values = values.at[chosen].set(top)
    values = values.at[(chosen + 1) % BURNERS].set(0)
    return values.astype(jnp.int32)


def shard_levels(key, extent, pieces, least, high):
    factor_of, own = 1.0, jax.random.fold_in(key, 6)
    for axis_at, parts in pieces:
        heights = jnp.exp(jax.random.uniform(jax.random.fold_in(own, axis_at), (parts,), jnp.float32, least / len(pieces), high / len(pieces)))
        factor_of = factor_of * jnp.repeat(heights, extent[axis_at] // parts).reshape([-1 if axis == axis_at else 1 for axis in range(len(extent))])
    return factor_of


def bell_draw(own_key, dims, width, bound, pieces=(), kind=jnp.bfloat16):
    factor_of = shard_levels(own_key, dims, pieces, -0.22, 0.18) if pieces else 1.0
    entries = jax.random.normal(own_key, dims, jnp.float32) * width * factor_of
    return jnp.minimum(jnp.maximum(entries, -bound), bound).astype(kind)


def setup_inputs(seed: int = 0) -> dict:
    seeds = jax.random.split(jax.random.key(seed), 8)
    density = jnp.clip(0.4 + 0.800000042 * jax.random.uniform(seeds[0], (NT, NR, NZ), jnp.float32) ** shard_levels(seeds[0], (NT, NR, NZ), ((0, 16), (1, 16)), -0.2, 0.2), 0.4, 1.2)
    swirl = bell_draw(seeds[1], (NT, NR, NZ), 1.0, 4.0, ((0, 16), (1, 16)), jnp.float32)
    heat_rate = jnp.clip(jnp.exp(math.log(3.0) - 3.4011974 * jax.random.uniform(seeds[2], (NT, NR, NZ), jnp.float32) ** shard_levels(seeds[2], (NT, NR, NZ), ((0, 16), (1, 16)), -0.2, 0.2)), 0.1, 3.0)
    acoustic = bell_draw(seeds[3], (3, NT, NZ), 1.0, 5.0, ((1, 16),), jnp.float32)
    mode_impedance = jnp.clip(jnp.exp(jax.random.uniform(seeds[4], (NT // 2 + 1,), jnp.float32, math.log(0.05), math.log(8.0))), 0.05, 8.0)
    mouth_azimuth = draw_mouth_azimuth(jax.random.fold_in(seeds[7], 71), 0)
    mouth_radius = draw_mouth_radius(jax.random.fold_in(seeds[7], 71), 0)
    return dict(density=density, swirl=swirl, heat_rate=heat_rate, acoustic=acoustic, mode_impedance=mode_impedance, mouth_azimuth=mouth_azimuth, mouth_radius=mouth_radius)


time_step = 0.2
diffusion = 0.05
inflow_rate = 0.5
wave_speed = 0.5
heat_coupling = 0.5
feedback = 0.5


def axial_pair(field):
    zeros = jnp.zeros_like(field[:, :, :1])
    return jnp.concatenate([field[:, :, 1:], zeros], 2) + jnp.concatenate([zeros, field[:, :, :-1]], 2)


def jacobi(forcing, diagonal):
    solution = forcing / diagonal
    for sweep in range(SWEEPS - 1):
        padded = jnp.pad(solution, ((0, 0), (1, 1), (0, 0)))
        solution = (forcing + (padded[:, 2:] + padded[:, :-2]) + axial_pair(solution)) / diagonal
    return solution


def reference(density, swirl, heat_rate, acoustic, mode_impedance, mouth_azimuth, mouth_radius):
    theta = jnp.arange(NT, dtype=jnp.int32)
    radius = jnp.arange(NR, dtype=jnp.int32)
    theta_start = jnp.arange(BURNERS, dtype=jnp.int32) * (NT // BURNERS) + mouth_azimuth
    inside_theta = ((theta[None, :] >= theta_start[:, None]) & (theta[None, :] < theta_start[:, None] + MOUTH)).astype(jnp.float32)
    inside_radius = ((radius[None, :] >= mouth_radius[:, None]) & (radius[None, :] < mouth_radius[:, None] + MOUTH)).astype(jnp.float32)
    mouth_mask = jnp.dot(inside_theta.T, inside_radius, preferred_element_type=jnp.float32)

    heat_field = heat_rate * density * density
    source = jnp.sum(heat_field, axis=1) / NR

    wave_press, wave_along, wave_axial = acoustic[0], acoustic[1], acoustic[2]
    zeros = jnp.zeros_like(wave_press[:, :1])
    for substep in range(SUBSTEPS):
        press_up = jnp.roll(wave_press, -1, axis=0)
        press_axial = jnp.concatenate([wave_press[:, 1:], zeros], 1)
        wave_along = wave_along - wave_speed * (press_up - wave_press)
        wave_axial = wave_axial - wave_speed * (press_axial - wave_press)
        along_down = jnp.roll(wave_along, 1, axis=0)
        axial_down = jnp.concatenate([zeros, wave_axial[:, :-1]], 1)
        wave_press = wave_press - wave_speed * ((wave_along - along_down) + (wave_axial - axial_down)) + heat_coupling * source
    acoustic_next = jnp.stack([wave_press, wave_along, wave_axial])

    flux = swirl * density
    twice = 2.0 * density
    radial_pad = jnp.pad(density, ((0, 0), (1, 1), (0, 0)))
    laplace = (jnp.roll(density, -1, axis=0) + jnp.roll(density, 1, axis=0) - twice) + (radial_pad[:, 2:] + radial_pad[:, :-2] - twice) + (axial_pair(density) - twice)
    advection = -0.5 * (jnp.roll(flux, -1, axis=0) - jnp.roll(flux, 1, axis=0))
    density_next = density + time_step * (advection + diffusion * laplace) + inflow_rate * mouth_mask[:, :, None] * (1.0 - density)
    forcing = (density_next - density) / time_step + feedback * wave_press[:, None, :]

    spectrum = jnp.fft.rfft(forcing, axis=0)
    order = jnp.arange(NT // 2 + 1, dtype=jnp.int32)
    shifted = 2.0 - 2.0 * jnp.cos(order.astype(jnp.float32) * (2.0 * math.pi / NT))
    diagonal = (4.0 + shifted + mode_impedance)[:, None, None]
    cosine = jacobi(jnp.real(spectrum).astype(jnp.float32), diagonal)
    sine = jacobi((-jnp.imag(spectrum)).astype(jnp.float32), diagonal)
    pressure = jnp.fft.irfft(cosine - 1j * sine, n=NT, axis=0).astype(jnp.float32)
    return density_next, pressure, acoustic_next
```

```python
import math

import jax
import jax.numpy as jnp
import numpy as np
from jax import lax
from jax.experimental import pallas as pl
from jax.experimental.pallas import tpu as pltpu
from jax.sharding import PartitionSpec as P

MOUTH = 8
SWEEPS = 4
SUBSTEPS = 8
REACH = SWEEPS - 1
NT, NR, NZ = 2048, 256, 128
SECTORS, RADIALS = 16, 16
T = NT // SECTORS
R = NR // RADIALS
Q = NZ // SECTORS
TILES = 8
WIDE = 2 * T
CHUNKS = ((0, 4), (12, 4), (4, 4), (8, 4))

F32, BF16 = jnp.float32, jnp.bfloat16


def halves(table):
    high = table.astype(BF16)
    low = (table - high.astype(np.float64)).astype(BF16)
    return np.stack([high, low])


def mode_tables():
    j = np.arange(T)
    a = np.arange(T)
    tiles = np.zeros((TILES, WIDE, WIDE))
    mode = np.zeros((TILES, WIDE), np.int64)
    for k in range(1, TILES):
        order = SECTORS * a + k
        phase = 2 * np.pi * ((j[:, None] * order[None, :]) % NT) / NT
        tiles[k, :T, :T], tiles[k, :T, T:] = np.cos(phase), np.sin(phase)
        tiles[k, T:, :T], tiles[k, T:, T:] = -np.sin(phase), np.cos(phase)
        mode[k] = np.concatenate([order, order])
    low_cos, low_sin = SECTORS * np.arange(T // 2 + 1), SECTORS * np.arange(1, T // 2)
    mid = SECTORS * np.arange(T // 2) + SECTORS // 2

    def phase_of(order):
        return 2 * np.pi * ((j[:, None] * order[None, :]) % NT) / NT

    tiles[0, :T, :T] = np.concatenate([np.cos(phase_of(low_cos)), np.sin(phase_of(low_sin))], 1)
    tiles[0, T:, T:] = np.concatenate([np.cos(phase_of(mid)), np.sin(phase_of(mid))], 1)
    mode[0] = np.concatenate([low_cos, low_sin, mid, mid])
    mode = np.minimum(mode, NT - mode)
    weight = np.where((mode == 0) | (mode == NT // 2), 1.0, 2.0) / NT
    return tiles, mode.reshape(-1), weight.reshape(-1)


def axial_tables():
    n = np.arange(1, NZ + 1)
    sines = math.sqrt(2.0 / (NZ + 1)) * np.sin(np.pi * ((n[:, None] * n[None, :]) % (2 * (NZ + 1))) / (NZ + 1))
    return sines, 2.0 * np.cos(np.pi * n / (NZ + 1))


C1, C2, C3 = (math.cos(math.pi * n / 8) for n in (1, 2, 3))


def cosine_stage(e):
    f = [e[n] + e[8 - n] for n in range(4)] + [e[4]]
    g = [e[n] - e[8 - n] for n in range(4)]
    outer, inner = f[0] + f[4], f[1] + f[3]
    differ, h = f[0] - f[4], C2 * (f[1] - f[3])
    both = outer + f[2]
    w = C2 * g[2]
    up, down = g[0] + w, g[0] - w
    b, c = C1 * g[1] + C3 * g[3], C3 * g[1] - C1 * g[3]
    return [both + inner, up + b, differ + h, down + c, outer - f[2], down - c, differ - h, up - b, both - inner]


def sine_stage(o):
    u = [None] + [o[n] + o[8 - n] for n in (1, 2, 3)] + [o[4]]
    v = [None] + [o[n] - o[8 - n] for n in (1, 2, 3)]
    h = C2 * (v[1] + v[3])
    w = C2 * u[2]
    up, down = w + u[4], w - u[4]
    b, c = C3 * u[1] + C1 * u[3], C1 * u[1] - C3 * u[3]
    return [None, b + up, h + v[2], c + down, v[1] - v[3], c - down, h - v[2], b - up]


def split(x):
    high = x.astype(BF16)
    return high, (x - high.astype(F32)).astype(BF16)


def product(left, right, dims=((1,), (0,))):
    def one(a, b):
        return lax.dot_general(a, b, (dims, ((), ())), preferred_element_type=F32)

    return one(left[0], right[0]) + (one(left[0], right[1]) + one(left[1], right[0]))


def rows_of(r):
    return pl.ds(r, T, stride=R)


def kernel(
    azimuth, radius, dens_hbm, swirl_hbm, heat_hbm, ac_hbm, inverse, lam, sines, fwd_hbm, bwd_hbm,
    dn_hbm, press_hbm, acn_hbm,
    dext, sext, heat, acx, hext, rsend, rhalo, tmask, srcbuf, agbuf, acn, psend, precv, phat,
    send1, recv1, send2, recv2, modes, yhi, ylo, xhi, xlo, zbuf, dn, press, fwd, bwd,
    load_sem, store_sem, halo_s, halo_r, rs_s, rs_r, ag_s, ag_r, pq_s, pq_r, f_s, f_r, b_s, b_r,
):
    s, rho = lax.axis_index("sector"), lax.axis_index("radial")
    after, before = lax.rem(s + 1, SECTORS), lax.rem(s + SECTORS - 1, SECTORS)
    inner, outer = lax.rem(rho + RADIALS - 1, RADIALS), lax.rem(rho + 1, RADIALS)

    def remote(src, dst, send, recv, **where):
        return pltpu.make_async_remote_copy(
            src_ref=src, dst_ref=dst, send_sem=send, recv_sem=recv, device_id=where, device_id_type=pl.DeviceIdType.MESH
        )

    def others(body):
        def step(i, carry):
            body(i)
            return carry

        lax.fori_loop(1, SECTORS, step, 0)

    loads = [
        pltpu.make_async_copy(dens_hbm, dext.at[pl.ds(R, T * R)], load_sem.at[0]),
        pltpu.make_async_copy(heat_hbm, heat, load_sem.at[1]),
        pltpu.make_async_copy(swirl_hbm, sext.at[pl.ds(R, T * R)], load_sem.at[2]),
        pltpu.make_async_copy(ac_hbm, acx.at[:, pl.ds(8, T)], load_sem.at[3]),
        pltpu.make_async_copy(fwd_hbm, fwd, load_sem.at[4]),
        pltpu.make_async_copy(bwd_hbm, bwd, load_sem.at[5]),
    ]
    for load in loads:
        load.start()

    barrier = pltpu.get_barrier_semaphore()

    def greet(i):
        pl.semaphore_signal(barrier, inc=1, device_id={"sector": lax.rem(s + i, SECTORS)}, device_id_type=pl.DeviceIdType.MESH)
        pl.semaphore_signal(barrier, inc=1, device_id={"radial": lax.rem(rho + i, RADIALS)}, device_id_type=pl.DeviceIdType.MESH)

    others(greet)
    pl.semaphore_wait(barrier, 2 * (SECTORS - 1))

    head, tail = pl.ds(0, R), pl.ds(T * R + R, R)
    azimuth_halos = [
        remote(dens_hbm.at[pl.ds(0, R)], dext.at[tail], halo_s.at[0], halo_r.at[0], sector=before),
        remote(dens_hbm.at[pl.ds(T * R - R, R)], dext.at[head], halo_s.at[1], halo_r.at[1], sector=after),
        remote(swirl_hbm.at[pl.ds(0, R)], sext.at[tail], halo_s.at[2], halo_r.at[2], sector=before),
        remote(swirl_hbm.at[pl.ds(T * R - R, R)], sext.at[head], halo_s.at[3], halo_r.at[3], sector=after),
    ]
    wave_halos = [
        remote(ac_hbm.at[:, pl.ds(0, 8)], acx.at[:, pl.ds(T + 8, 8)], halo_s.at[4], halo_r.at[4], sector=before),
        remote(ac_hbm.at[:, pl.ds(T - 8, 8)], acx.at[:, pl.ds(0, 8)], halo_s.at[5], halo_r.at[5], sector=after),
    ]
    for copy in azimuth_halos:
        copy.start()

    loads[0].wait()
    to_inner = remote(rsend.at[0], rhalo.at[1], halo_s.at[6], halo_r.at[6], radial=inner)
    to_outer = remote(rsend.at[1], rhalo.at[0], halo_s.at[7], halo_r.at[7], radial=outer)
    rsend[0] = dext[pl.ds(R, T, stride=R), :]
    rsend[1] = dext[pl.ds(2 * R - 1, T, stride=R), :]

    @pl.when(rho > 0)
    def _():
        to_inner.start()

    @pl.when(rho < RADIALS - 1)
    def _():
        to_outer.start()

    for copy in wave_halos:
        copy.start()

    loads[1].wait()

    def heat_row(r, total):
        d = dext[pl.ds(R + r, T, stride=R), :]
        return total + heat[rows_of(r), :] * d * d

    hext[8 : 8 + T, :] = lax.fori_loop(0, R, heat_row, jnp.zeros((T, NZ), F32)) * (1.0 / NR)
    heat_halos = [
        remote(hext.at[pl.ds(8, 8)], hext.at[pl.ds(T + 8, 8)], halo_s.at[8], halo_r.at[8], sector=before),
        remote(hext.at[pl.ds(T, 8)], hext.at[pl.ds(0, 8)], halo_s.at[9], halo_r.at[9], sector=after),
    ]
    for copy in heat_halos:
        copy.start()

    theta = lax.broadcasted_iota(jnp.int32, (T, NZ), 0)
    first = azimuth[s]
    tmask[...] = jnp.where((theta >= first) & (theta < first + MOUTH), 1.0, 0.0).astype(F32)
    lane = lax.broadcasted_iota(jnp.int32, (T, NZ), 1)
    loads[2].wait()
    for copy in azimuth_halos:
        copy.wait_recv()

    @pl.when(rho > 0)
    def _():
        to_outer.wait_recv()

    @pl.when(rho == 0)
    def _():
        rhalo[0] = jnp.zeros((T, NZ), F32)

    @pl.when(rho < RADIALS - 1)
    def _():
        to_inner.wait_recv()

    @pl.when(rho == RADIALS - 1)
    def _():
        rhalo[1] = jnp.zeros((T, NZ), F32)

    sine_pair = (sines[0], sines[1])

    def flow_row(r, below, above):
        d = dext[pl.ds(R + r, T, stride=R), :]
        up = dext[pl.ds(2 * R + r, T, stride=R), :]
        down = dext[pl.ds(r, T, stride=R), :]
        axial = jnp.where(lane < NZ - 1, pltpu.roll(d, NZ - 1, 1), 0.0) + jnp.where(lane > 0, pltpu.roll(d, 1, 1), 0.0)
        laplace = (up + down) + (below + above) + axial - 6.0 * d
        flux = sext[pl.ds(2 * R + r, T, stride=R), :] * up - sext[pl.ds(r, T, stride=R), :] * down
        where = rho * R + r - radius[s]
        mouth = jnp.where((where >= 0) & (where < MOUTH), 2.5, 0.0).astype(F32)
        change = 0.05 * laplace - 0.5 * flux + (mouth * tmask[...]) * (1.0 - d)
        dn[rows_of(r), :] = d + 0.2 * change
        lines = product(sine_pair, split(change), ((1,), (1,)))
        send1[:, r] = lines.reshape(SECTORS, Q, T)

    def flow_inside(r, carry):
        flow_row(r, dext[pl.ds(R + r - 1, T, stride=R), :], dext[pl.ds(R + r + 1, T, stride=R), :])
        return carry

    def flow_chunk(c):
        start, count = CHUNKS[c]
        lo, hi = max(start, 1), min(start + count, R - 1)
        if start == 0:
            flow_row(0, rhalo[0], dext[pl.ds(R + 1, T, stride=R), :])
        lax.fori_loop(lo, hi, flow_inside, 0)
        if start + count == R:
            flow_row(R - 1, dext[pl.ds(2 * R - 2, T, stride=R), :], rhalo[1])
        part = pl.ds(start, count)
        others(
            lambda i: remote(
                send1.at[lax.rem(s + i, SECTORS), part], recv1.at[s, part], f_s.at[c, lax.rem(s + i, SECTORS)], f_r.at[c, s],
                sector=lax.rem(s + i, SECTORS),
            ).start()
        )
        recv1[s, part] = send1[s, part]

    def tile_rows(peer):
        return pl.ds(pl.multiple_of(8 * peer, 8), 24)

    def share_heat(i):
        peer = lax.rem(rho + i, RADIALS)
        return remote(hext.at[tile_rows(peer)], srcbuf.at[rho], rs_s.at[peer], rs_r.at[rho], radial=peer)

    def share_wave(i):
        peer = lax.rem(rho + i, RADIALS)
        return remote(agbuf.at[rho], agbuf.at[rho], ag_s.at[peer], ag_r.at[rho], radial=peer)

    def share_press(i):
        peer = lax.rem(s + i, SECTORS)
        return remote(psend.at[peer], precv.at[s], pq_s.at[peer], pq_r.at[s], sector=peer)

    flow_chunk(0)

    for copy in heat_halos + wave_halos:
        copy.wait_recv()
    loads[3].wait()
    others(lambda i: share_heat(i).start())
    srcbuf[rho] = hext[tile_rows(rho), :]

    flow_chunk(1)

    def arrived(buffer, send, recv, index, **where):
        remote(buffer, buffer, send, recv.at[index], **where).wait_recv()

    def heat_in(i):
        peer = lax.rem(rho + i, RADIALS)
        arrived(srcbuf.at[peer], rs_s.at[peer], rs_r, peer, radial=peer)

    others(heat_in)
    source = srcbuf[0]
    for i in range(1, RADIALS):
        source = source + srcbuf[i]
    source = 0.5 * source
    wave = [acx[n, tile_rows(rho), :] for n in range(3)]
    lane24 = lax.broadcasted_iota(jnp.int32, (24, NZ), 1)
    p, u, w = wave
    for _ in range(SUBSTEPS):
        u = u - 0.5 * (pltpu.roll(p, 23, 0) - p)
        w = w - 0.5 * (jnp.where(lane24 < NZ - 1, pltpu.roll(p, NZ - 1, 1), 0.0) - p)
        along, axial = u - pltpu.roll(u, 1, 0), w - jnp.where(lane24 > 0, pltpu.roll(w, 1, 1), 0.0)
        p = p - 0.5 * (along + axial) + source
    for n, field in enumerate((p, u, w)):
        agbuf[rho, n] = field[8:16]
    others(lambda i: share_wave(i).start())

    flow_chunk(2)

    def wave_in(i):
        peer = lax.rem(rho + i, RADIALS)
        arrived(agbuf.at[peer], ag_s.at[peer], ag_r, peer, radial=peer)

    others(wave_in)
    for n in range(3):
        acn[n] = agbuf[:, n].reshape(T, NZ)
    stores = [
        pltpu.make_async_copy(acn, acn_hbm, store_sem.at[0]),
        pltpu.make_async_copy(dn, dn_hbm, store_sem.at[1]),
        pltpu.make_async_copy(press, press_hbm, store_sem.at[2]),
    ]
    stores[0].start()
    psend[...] = product(sine_pair, split(0.5 * acn[0]), ((1,), (1,))).reshape(SECTORS, Q, T)
    others(lambda i: share_press(i).start())
    precv[s] = psend[s]

    flow_chunk(3)
    stores[1].start()
    loads[4].wait()

    def first_stage(x):
        e = [x[0]] + [x[n] + x[SECTORS - n] for n in range(1, 8)] + [x[8]]
        o = [None] + [x[n] - x[SECTORS - n] for n in range(1, 8)]
        return cosine_stage(e), sine_stage(o)

    def keep(row, values):
        cosines, sines_ = values
        at = pl.ds(row, 2 * Q)
        for k in range(TILES):
            pair = (cosines[0], cosines[8]) if k == 0 else (cosines[k], sines_[k])
            for half, value in enumerate(pair):
                high, low = split(value)
                yhi[k, at, T * half : T * half + T] = high
                ylo[k, at, T * half : T * half + T] = low

    def second_stage(rows, table, k):
        return product((yhi[k, rows, :], ylo[k, rows, :]), (table[0, k], table[1, k]))

    def mode_lanes(k):
        return pl.ds(pl.multiple_of(k * WIDE, WIDE), WIDE)

    def forward_chunk(c):
        start, count = CHUNKS[c]
        part = pl.ds(start, count)

        def lines_in(i):
            peer = lax.rem(s + i, SECTORS)
            arrived(recv1.at[peer, part], f_s.at[c, peer], f_r, (c, peer), sector=peer)

        others(lines_in)

        def pair(i, carry):
            r = start + 2 * i
            x = [recv1[n, pl.ds(r, 2)].reshape(2 * Q, T) for n in range(SECTORS)]
            keep(pl.multiple_of(r * Q, 2 * Q), first_stage(x))
            return carry

        lax.fori_loop(0, count // 2, pair, 0)

        def tile(k, carry):
            out = second_stage(pl.ds(start * Q, count * Q), fwd, k)
            modes[pl.ds(REACH + start, count), :, mode_lanes(k)] = out.reshape(count, Q, WIDE)
            return carry

        lax.fori_loop(0, TILES, tile, 0)

    modes_inner = remote(modes.at[pl.ds(REACH, REACH)], modes.at[pl.ds(REACH + R, REACH)], halo_s.at[10], halo_r.at[10], radial=inner)
    modes_outer = remote(modes.at[pl.ds(R, REACH)], modes.at[pl.ds(0, REACH)], halo_s.at[11], halo_r.at[11], radial=outer)

    forward_chunk(0)

    @pl.when(rho > 0)
    def _():
        modes_inner.start()

    forward_chunk(1)

    @pl.when(rho < RADIALS - 1)
    def _():
        modes_outer.start()

    forward_chunk(2)
    forward_chunk(3)

    def press_in(i):
        peer = lax.rem(s + i, SECTORS)
        arrived(precv.at[peer], pq_s.at[peer], pq_r, peer, sector=peer)

    others(press_in)
    both = [jnp.concatenate([precv[n], precv[n]], 0) for n in range(SECTORS)]
    keep(T, first_stage(both))

    def press_tile(k, carry):
        phat[:, mode_lanes(k)] = second_stage(pl.ds(T, 2 * Q), fwd, k)[:Q]
        return carry

    lax.fori_loop(0, TILES, press_tile, 0)

    @pl.when(rho > 0)
    def _():
        modes_outer.wait_recv()

    @pl.when(rho == 0)
    def _():
        modes[0:REACH] = jnp.zeros((REACH, Q, NT), F32)

    @pl.when(rho < RADIALS - 1)
    def _():
        modes_inner.wait_recv()

    @pl.when(rho == RADIALS - 1)
    def _():
        modes[REACH + R : R + 2 * REACH] = jnp.zeros((REACH, Q, NT), F32)

    axial_sum = lam[pl.ds(pl.multiple_of(s * Q, Q), Q), :]
    keep_low = jnp.where(rho > 0, 1.0, 0.0).astype(F32)
    keep_high = jnp.where(rho < RADIALS - 1, 1.0, 0.0).astype(F32)

    def solve(block, carry):
        at = pl.ds(pl.multiple_of(block * T, T), T)
        inv = jnp.broadcast_to(inverse[0:1, at], (Q, T))
        last = jnp.broadcast_to(inverse[1:2, at], (Q, T))
        total = R + 2 * REACH
        scale = [inv * keep_low] * REACH + [inv] * R + [inv * keep_high] * REACH
        extra = phat[:, at]
        ends = [extra * keep_low] * REACH + [extra] * R + [extra * keep_high] * REACH
        c = [modes[n, :, at] + ends[n] for n in range(total)]
        x = [c[n] * scale[n] for n in range(total)]
        for sweep in range(1, SWEEPS):
            x = [
                None
                if n < sweep or n >= total - sweep
                else ((c[n] + axial_sum * x[n]) + (x[n - 1] + x[n + 1])) * (last if sweep == SWEEPS - 1 else scale[n])
                for n in range(total)
            ]
        for n in range(0, R, 2):
            high, low = split(jnp.concatenate([x[REACH + n], x[REACH + n + 1]], 0))
            xhi[n * Q : n * Q + 2 * Q, at] = high
            xlo[n * Q : n * Q + 2 * Q, at] = low
        return carry

    lax.fori_loop(0, NT // T, solve, 0)
    loads[5].wait()

    def backward_chunk(c):
        start, count = CHUNKS[c]
        rows, part = pl.ds(start * Q, count * Q), pl.ds(start, count)

        def tile(k, carry):
            at = mode_lanes(k)
            zbuf[k, rows, :] = product((xhi[rows, at], xlo[rows, at]), (bwd[0, k], bwd[1, k]))
            return carry

        lax.fori_loop(0, TILES, tile, 0)

        def row(i, carry):
            r = start + i
            at = pl.ds(pl.multiple_of(r * Q, Q), Q)
            z = [(zbuf[k, at, 0:T], zbuf[k, at, T:WIDE]) for k in range(TILES)]
            even = cosine_stage([z[0][0]] + [z[k][0] for k in range(1, TILES)] + [z[0][1]])
            odd = sine_stage([None] + [z[k][1] for k in range(1, TILES)])
            send2[0, r], send2[8, r] = even[0], even[8]
            for n in range(1, 8):
                send2[n, r] = even[n] + odd[n]
                send2[SECTORS - n, r] = even[n] - odd[n]
            return carry

        lax.fori_loop(0, count, row, 0)
        others(
            lambda i: remote(
                send2.at[lax.rem(s + i, SECTORS), part], recv2.at[s, part], b_s.at[c, lax.rem(s + i, SECTORS)], b_r.at[c, s],
                sector=lax.rem(s + i, SECTORS),
            ).start()
        )
        recv2[s, part] = send2[s, part]

    for c in range(len(CHUNKS)):
        backward_chunk(c)

    for c, (start, count) in enumerate(CHUNKS):
        part = pl.ds(start, count)

        def lines_back(i, c=c, part=part):
            peer = lax.rem(s + i, SECTORS)
            arrived(recv2.at[peer, part], b_s.at[c, peer], b_r, (c, peer), sector=peer)

        others(lines_back)

        def finish(r, carry):
            lines = recv2[:, r].reshape(NZ, T).T
            press[rows_of(r), :] = product(split(lines), sine_pair)
            return carry

        lax.fori_loop(start, start + count, finish, 0)
    stores[2].start()

    for copy in azimuth_halos + wave_halos + heat_halos:
        copy.wait_send()

    @pl.when(rho > 0)
    def _():
        to_inner.wait_send()
        modes_inner.wait_send()

    @pl.when(rho < RADIALS - 1)
    def _():
        to_outer.wait_send()
        modes_outer.wait_send()

    def sent(i):
        share_heat(i).wait_send()
        share_wave(i).wait_send()
        share_press(i).wait_send()
        peer = lax.rem(s + i, SECTORS)
        for c, (start, count) in enumerate(CHUNKS):
            part = pl.ds(start, count)
            remote(send1.at[peer, part], recv1.at[s, part], f_s.at[c, peer], f_r.at[c, s], sector=peer).wait_send()
            remote(send2.at[peer, part], recv2.at[s, part], b_s.at[c, peer], b_r.at[c, s], sector=peer).wait_send()

    others(sent)
    for store in stores:
        store.wait()


def shards(density, swirl, heat_rate, acoustic, mode_impedance, mouth_azimuth, mouth_radius):
    tiles, mode, weight = mode_tables()
    sines, axial_sum = axial_tables()
    half = NT // 2
    whole = jnp.concatenate([mode_impedance, mode_impedance[1:half][::-1]]).reshape(T, SECTORS).T
    by_lane = jnp.concatenate(
        [whole[0, : T // 2 + 1], whole[0, 1 : T // 2], whole[8, : T // 2], whole[8, : T // 2]]
        + [whole[k] for k in range(1, TILES) for _ in range(2)]
    )
    diagonal = jnp.asarray((4.0 + 2.0 - 2.0 * np.cos(2 * np.pi * mode / NT)).astype(np.float32)) + by_lane
    inverse = 1.0 / diagonal
    inverse = jnp.stack([inverse, inverse * jnp.asarray(weight.astype(np.float32))])
    lam = jnp.asarray(np.repeat(axial_sum[:, None], T, 1).astype(np.float32))
    flat = lambda x: x.reshape(T * R, NZ)
    vmem, smem, anywhere = (pl.BlockSpec(memory_space=m) for m in (pltpu.VMEM, pltpu.SMEM, pl.ANY))
    dma = pltpu.SemaphoreType.DMA
    dn, press, acn = pl.pallas_call(
        kernel,
        out_shape=(
            jax.ShapeDtypeStruct((T * R, NZ), F32),
            jax.ShapeDtypeStruct((T * R, NZ), F32),
            jax.ShapeDtypeStruct((3, T, NZ), F32),
        ),
        in_specs=[smem, smem] + [anywhere] * 4 + [vmem] * 3 + [anywhere] * 2,
        out_specs=(anywhere, anywhere, anywhere),
        scratch_shapes=[
            pltpu.VMEM(((T + 2) * R, NZ), F32),
            pltpu.VMEM(((T + 2) * R, NZ), F32),
            pltpu.VMEM((T * R, NZ), F32),
            pltpu.VMEM((3, T + 16, NZ), F32),
            pltpu.VMEM((T + 16, NZ), F32),
            pltpu.VMEM((2, T, NZ), F32),
            pltpu.VMEM((2, T, NZ), F32),
            pltpu.VMEM((T, NZ), F32),
            pltpu.VMEM((RADIALS, 24, NZ), F32),
            pltpu.VMEM((RADIALS, 3, 8, NZ), F32),
            pltpu.VMEM((3, T, NZ), F32),
            pltpu.VMEM((SECTORS, Q, T), F32),
            pltpu.VMEM((SECTORS, Q, T), F32),
            pltpu.VMEM((Q, NT), F32),
            pltpu.VMEM((SECTORS, R, Q, T), F32),
            pltpu.VMEM((SECTORS, R, Q, T), F32),
            pltpu.VMEM((SECTORS, R, Q, T), F32),
            pltpu.VMEM((SECTORS, R, Q, T), F32),
            pltpu.VMEM((R + 2 * REACH, Q, NT), F32),
            pltpu.VMEM((TILES, R * Q + 2 * Q, WIDE), BF16),
            pltpu.VMEM((TILES, R * Q + 2 * Q, WIDE), BF16),
            pltpu.VMEM((R * Q, NT), BF16),
            pltpu.VMEM((R * Q, NT), BF16),
            pltpu.VMEM((TILES, R * Q, WIDE), F32),
            pltpu.VMEM((T * R, NZ), F32),
            pltpu.VMEM((T * R, NZ), F32),
            pltpu.VMEM((2, TILES, WIDE, WIDE), BF16),
            pltpu.VMEM((2, TILES, WIDE, WIDE), BF16),
            dma((6,)),
            dma((3,)),
            dma((12,)),
            dma((12,)),
            dma((RADIALS,)),
            dma((RADIALS,)),
            dma((RADIALS,)),
            dma((RADIALS,)),
            dma((SECTORS,)),
            dma((SECTORS,)),
            dma((len(CHUNKS), SECTORS)),
            dma((len(CHUNKS), SECTORS)),
            dma((len(CHUNKS), SECTORS)),
            dma((len(CHUNKS), SECTORS)),
        ],
        compiler_params=pltpu.CompilerParams(collective_id=0, has_side_effects=True, vmem_limit_bytes=48 * 2**20),
    )(
        mouth_azimuth, mouth_radius, flat(density), flat(swirl), flat(heat_rate), acoustic, inverse, lam,
        jnp.asarray(halves(sines)), jnp.asarray(halves(tiles)), jnp.asarray(halves(tiles.transpose(0, 2, 1))),
    )
    return dn.reshape(T, R, NZ), press.reshape(T, R, NZ), acn


def solution(mesh):
    cells, columns = P("sector", "radial", None), P(None, "sector", None)
    return jax.shard_map(
        shards,
        mesh=mesh,
        in_specs=(cells, cells, cells, columns, P(), P(), P()),
        out_specs=(cells, cells, columns),
        check_vma=False,
    )
```

```python
import math

import jax
import jax.numpy as jnp
import numpy as np
from jax import lax
from jax.experimental import pallas as pl
from jax.experimental.pallas import tpu as pltpu
from jax.sharding import PartitionSpec as P

MOUTH = 8
SWEEPS = 4
SUBSTEPS = 8
REACH = SWEEPS - 1
NT, NR, NZ = 2048, 256, 128
SECTORS, RADIALS = 16, 16
T = NT // SECTORS
R = NR // RADIALS
Q = NZ // SECTORS
TILES = 8
WIDE = 2 * T
BURNERS = 16
EDGE = 4
SENDS = ((0, 4), (4, 4), (8, 4), (12, 4))
RETURNS = ((0, 4), (4, 6), (10, 4), (14, 2))
VMEM_LIMIT = 48 * 2**20

F32, BF16 = jnp.float32, jnp.bfloat16


def halves(table):
    high = table.astype(BF16)
    low = (table - high.astype(np.float64)).astype(BF16)
    return np.stack([high, low])


def mode_tables():
    j = np.arange(T)
    a = np.arange(T)
    tiles = np.zeros((TILES, WIDE, WIDE))
    mode = np.zeros((TILES, WIDE), np.int64)
    for k in range(1, TILES):
        order = SECTORS * a + k
        phase = 2 * np.pi * ((j[:, None] * order[None, :]) % NT) / NT
        tiles[k, :T, :T], tiles[k, :T, T:] = np.cos(phase), np.sin(phase)
        tiles[k, T:, :T], tiles[k, T:, T:] = -np.sin(phase), np.cos(phase)
        mode[k] = np.concatenate([order, order])
    low_cos, low_sin = SECTORS * np.arange(T // 2 + 1), SECTORS * np.arange(1, T // 2)
    mid = SECTORS * np.arange(T // 2) + SECTORS // 2

    def phase_of(order):
        return 2 * np.pi * ((j[:, None] * order[None, :]) % NT) / NT

    tiles[0, :T, :T] = np.concatenate([np.cos(phase_of(low_cos)), np.sin(phase_of(low_sin))], 1)
    tiles[0, T:, T:] = np.concatenate([np.cos(phase_of(mid)), np.sin(phase_of(mid))], 1)
    mode[0] = np.concatenate([low_cos, low_sin, mid, mid])
    mode = np.minimum(mode, NT - mode)
    weight = np.where((mode == 0) | (mode == NT // 2), 1.0, 2.0) / NT
    return tiles, mode.reshape(-1), weight.reshape(-1)


def axial_tables():
    n = np.arange(1, NZ + 1)
    sines = math.sqrt(2.0 / (NZ + 1)) * np.sin(np.pi * ((n[:, None] * n[None, :]) % (2 * (NZ + 1))) / (NZ + 1))
    return sines, 2.0 * np.cos(np.pi * n / (NZ + 1))


C1, C2, C3 = (math.cos(math.pi * n / 8) for n in (1, 2, 3))


def cosine_stage(e):
    f = [e[n] + e[8 - n] for n in range(4)] + [e[4]]
    g = [e[n] - e[8 - n] for n in range(4)]
    outer, inner = f[0] + f[4], f[1] + f[3]
    differ, h = f[0] - f[4], C2 * (f[1] - f[3])
    both = outer + f[2]
    w = C2 * g[2]
    up, down = g[0] + w, g[0] - w
    b, c = C1 * g[1] + C3 * g[3], C3 * g[1] - C1 * g[3]
    return [both + inner, up + b, differ + h, down + c, outer - f[2], down - c, differ - h, up - b, both - inner]


def sine_stage(o):
    u = [None] + [o[n] + o[8 - n] for n in (1, 2, 3)] + [o[4]]
    v = [None] + [o[n] - o[8 - n] for n in (1, 2, 3)]
    h = C2 * (v[1] + v[3])
    w = C2 * u[2]
    up, down = w + u[4], w - u[4]
    b, c = C3 * u[1] + C1 * u[3], C1 * u[1] - C3 * u[3]
    return [None, b + up, h + v[2], c + down, v[1] - v[3], c - down, h - v[2], b - up]


def split(x):
    high = x.astype(BF16)
    return high, (x - high.astype(F32)).astype(BF16)


def product(left, right, dims=((1,), (0,))):
    def one(a, b):
        return lax.dot_general(a, b, (dims, ((), ())), preferred_element_type=F32)

    return one(left[0], right[0]) + (one(left[0], right[1]) + one(left[1], right[0]))


def stacked(ref, rows, half, lanes, right):
    both = lax.dot_general(ref[rows, lanes], right[0], (((1,), (0,)), ((), ())), preferred_element_type=F32)
    high = ref[pl.ds(rows.start, half), lanes]
    return both[:half] + (both[half:] + lax.dot_general(high, right[1], (((1,), (0,)), ((), ())), preferred_element_type=F32))


def kernel(
    azimuth_hbm, radius_hbm, impedance, dens_hbm, swirl_hbm, heat_hbm, ac_hbm, lam_hbm, sines_hbm, pick_hbm, base_hbm, fwd_hbm, bwd_hbm,
    dn, press, acn,
    azimuth, radius, dext, sext, heat, dr, acx, hext, tmask, srcbuf, agbuf, psend, precv, phat,
    send1, recv1, send2, recv2, modes, y, x2, zbuf, inverse, lam, sines, pick, base, fwd, bwd,
    load_sem, halo_s, halo_r, few_s, few_r, f_s, f_r, b_s, b_r,
):
    s, rho = lax.axis_index("sector"), lax.axis_index("radial")
    after, before = lax.rem(s + 1, SECTORS), lax.rem(s + SECTORS - 1, SECTORS)
    inner, outer = lax.rem(rho + RADIALS - 1, RADIALS), lax.rem(rho + 1, RADIALS)
    sine_rest = pl.ds(0, SECTORS - 1)

    def remote(src, dst, send, recv, **where):
        return pltpu.make_async_remote_copy(
            src_ref=src, dst_ref=dst, send_sem=send, recv_sem=recv, device_id=where, device_id_type=pl.DeviceIdType.MESH
        )

    def others(body):
        def step(i, carry):
            body(i)
            return carry

        lax.fori_loop(1, SECTORS, step, 0)

    loads = [
        pltpu.make_async_copy(src, dst, load_sem.at[n])
        for n, (src, dst) in enumerate(
            [
                (dens_hbm, dext.at[pl.ds(R, T * R)]),
                (heat_hbm, heat),
                (swirl_hbm, sext.at[pl.ds(R, T * R)]),
                (azimuth_hbm, azimuth),
                (radius_hbm, radius),
                (sines_hbm, sines),
                (ac_hbm, acx.at[:, pl.ds(8, T)]),
                (lam_hbm, lam),
                (pick_hbm, pick),
                (base_hbm, base),
                (fwd_hbm, fwd),
                (bwd_hbm, bwd),
            ]
        )
    ]
    for load in loads:
        load.start()

    barrier = pltpu.get_barrier_semaphore()

    def greet(i):
        pl.semaphore_signal(barrier, inc=1, device_id={"sector": lax.rem(s + i, SECTORS)}, device_id_type=pl.DeviceIdType.MESH)
        pl.semaphore_signal(barrier, inc=1, device_id={"radial": lax.rem(rho + i, RADIALS)}, device_id_type=pl.DeviceIdType.MESH)

    others(greet)
    loads[0].wait()
    dr[1] = dext[pl.ds(R, T, stride=R), :]
    dr[R] = dext[pl.ds(2 * R - 1, T, stride=R), :]
    pl.semaphore_wait(barrier, 2 * (SECTORS - 1))

    head, tail = pl.ds(0, R), pl.ds(T * R + R, R)
    azimuth_halos = [
        remote(dens_hbm.at[pl.ds(0, R)], dext.at[tail], halo_s.at[0], halo_r.at[0], sector=before),
        remote(dens_hbm.at[pl.ds(T * R - R, R)], dext.at[head], halo_s.at[1], halo_r.at[1], sector=after),
        remote(swirl_hbm.at[pl.ds(0, R)], sext.at[tail], halo_s.at[2], halo_r.at[2], sector=before),
        remote(swirl_hbm.at[pl.ds(T * R - R, R)], sext.at[head], halo_s.at[3], halo_r.at[3], sector=after),
    ]
    wave_halos = [
        remote(ac_hbm.at[:, pl.ds(0, 8)], acx.at[:, pl.ds(T + 8, 8)], halo_s.at[4], halo_r.at[4], sector=before),
        remote(ac_hbm.at[:, pl.ds(T - 8, 8)], acx.at[:, pl.ds(0, 8)], halo_s.at[5], halo_r.at[5], sector=after),
    ]
    to_inner = remote(dr.at[1], dr.at[R + 1], halo_s.at[6], halo_r.at[6], radial=inner)
    to_outer = remote(dr.at[R], dr.at[0], halo_s.at[7], halo_r.at[7], radial=outer)
    for copy in azimuth_halos:
        copy.start()

    @pl.when(rho > 0)
    def _():
        to_inner.start()

    @pl.when(rho < RADIALS - 1)
    def _():
        to_outer.start()

    for copy in wave_halos:
        copy.start()

    loads[1].wait()

    def heat_row(r, total):
        d = dext[pl.ds(R + r, T, stride=R), :]
        dr[r + 1] = d
        return total + heat[pl.ds(r, T, stride=R), :] * d * d

    ends = heat[pl.ds(0, T, stride=R), :] * dr[1] * dr[1] + heat[pl.ds(R - 1, T, stride=R), :] * dr[R] * dr[R]
    hext[8 : 8 + T, :] = lax.fori_loop(1, R - 1, heat_row, ends) * (1.0 / NR)
    heat_halos = [
        remote(hext.at[pl.ds(8, 8)], hext.at[pl.ds(T + 8, 8)], halo_s.at[8], halo_r.at[8], sector=before),
        remote(hext.at[pl.ds(T, 8)], hext.at[pl.ds(0, 8)], halo_s.at[9], halo_r.at[9], sector=after),
    ]
    for copy in heat_halos:
        copy.start()

    for n in (3, 4, 5, 2):
        loads[n].wait()
    theta = lax.broadcasted_iota(jnp.int32, (T, NZ), 0)
    first = azimuth[s]
    tmask[...] = jnp.where((theta >= first) & (theta < first + MOUTH), 1.0, 0.0).astype(F32)
    lane = lax.broadcasted_iota(jnp.int32, (T, NZ), 1)
    for copy in azimuth_halos:
        copy.wait_recv()

    @pl.when(rho > 0)
    def _():
        to_outer.wait_recv()

    @pl.when(rho == 0)
    def _():
        dr[0] = jnp.zeros((T, NZ), F32)

    @pl.when(rho < RADIALS - 1)
    def _():
        to_inner.wait_recv()

    @pl.when(rho == RADIALS - 1)
    def _():
        dr[R + 1] = jnp.zeros((T, NZ), F32)

    sine_pair = (sines[0], sines[1])

    def flow_row(i, carry):
        r = lax.rem(i + R - EDGE, R)
        d = dr[r + 1]
        up = dext[pl.ds(2 * R + r, T, stride=R), :]
        down = dext[pl.ds(r, T, stride=R), :]
        axial = jnp.where(lane < NZ - 1, pltpu.roll(d, NZ - 1, 1), 0.0) + jnp.where(lane > 0, pltpu.roll(d, 1, 1), 0.0)
        laplace = (up + down) + (dr[r] + dr[r + 2]) + axial - 6.0 * d
        flux = sext[pl.ds(2 * R + r, T, stride=R), :] * up - sext[pl.ds(r, T, stride=R), :] * down
        where = rho * R + r - radius[s]
        mouth = jnp.where((where >= 0) & (where < MOUTH), 2.5, 0.0).astype(F32)
        change = 0.05 * laplace - 0.5 * flux + (mouth * tmask[...]) * (1.0 - d)
        dn[pl.ds(r, T, stride=R), :] = d + 0.2 * change
        lines = product(sine_pair, split(change), ((1,), (1,)))
        send1[:, i] = lines.reshape(SECTORS, Q, T)
        return carry

    def flow_chunk(c):
        start, count = SENDS[c]
        lax.fori_loop(start, start + count, flow_row, 0)
        part = pl.ds(start, count)

        def go(i):
            peer = lax.rem(s + i, SECTORS)
            remote(send1.at[peer, part], recv1.at[s, part], f_s.at[c], f_r.at[c], sector=peer).start()

        others(go)
        recv1[s, part] = send1[s, part]

    def forward_all(c):
        part = pl.ds(*SENDS[c])
        return remote(send1.at[sine_rest, part], recv1.at[sine_rest, part], f_s.at[c], f_r.at[c], sector=after)

    def backward_all(c):
        part = pl.ds(*RETURNS[c])
        return remote(send2.at[sine_rest, part], recv2.at[sine_rest, part], b_s.at[c], b_r.at[c], sector=after)

    def tile_rows(peer):
        return pl.ds(pl.multiple_of(8 * peer, 8), 24)

    def share_heat(i):
        peer = lax.rem(rho + i, RADIALS)
        remote(hext.at[tile_rows(peer)], srcbuf.at[rho], few_s.at[0], few_r.at[0], radial=peer).start()

    def share_wave(i):
        peer = lax.rem(rho + i, RADIALS)
        remote(agbuf.at[rho], agbuf.at[rho], few_s.at[1], few_r.at[1], radial=peer).start()

    def share_press(i):
        peer = lax.rem(s + i, SECTORS)
        remote(psend.at[peer], precv.at[s], few_s.at[2], few_r.at[2], sector=peer).start()

    all_heat = remote(srcbuf.at[sine_rest], srcbuf.at[sine_rest], few_s.at[0], few_r.at[0], radial=outer)
    all_wave = remote(agbuf.at[sine_rest], agbuf.at[sine_rest], few_s.at[1], few_r.at[1], radial=outer)
    all_press = remote(psend.at[sine_rest], precv.at[sine_rest], few_s.at[2], few_r.at[2], sector=after)

    flow_chunk(0)

    for copy in heat_halos + wave_halos:
        copy.wait_recv()
    others(share_heat)
    srcbuf[rho] = hext[tile_rows(rho), :]

    flow_chunk(1)

    loads[6].wait()
    all_heat.wait_recv()
    source = srcbuf[0]
    for i in range(1, RADIALS):
        source = source + srcbuf[i]
    source = 0.5 * source
    lane24 = lax.broadcasted_iota(jnp.int32, (24, NZ), 1)
    p, u, w = (acx[n, tile_rows(rho), :] for n in range(3))
    for _ in range(SUBSTEPS):
        u = u - 0.5 * (pltpu.roll(p, 23, 0) - p)
        w = w - 0.5 * (jnp.where(lane24 < NZ - 1, pltpu.roll(p, NZ - 1, 1), 0.0) - p)
        along, axial = u - pltpu.roll(u, 1, 0), w - jnp.where(lane24 > 0, pltpu.roll(w, 1, 1), 0.0)
        p = p - 0.5 * (along + axial) + source
    for n, field in enumerate((p, u, w)):
        agbuf[rho, n] = field[8:16]
    others(share_wave)

    flow_chunk(2)

    all_wave.wait_recv()
    for n in range(3):
        acn[n] = agbuf[:, n].reshape(T, NZ)
    psend[...] = product(sine_pair, split(0.5 * acn[0]), ((1,), (1,))).reshape(SECTORS, Q, T)
    others(share_press)
    precv[s] = psend[s]

    flow_chunk(3)

    for n in (7, 8, 9):
        loads[n].wait()
    whole = impedance[...]
    top = whole.astype(BF16)
    rest = whole - top.astype(F32)
    middle = rest.astype(BF16)
    bottom = (rest - middle.astype(F32)).astype(BF16)

    def diagonal_of(k, carry):
        at = pl.ds(pl.multiple_of(k * WIDE, WIDE), WIDE)
        picked = [
            lax.dot_general(part, pick[0:T, at], (((1,), (0,)), ((), ())), preferred_element_type=F32) for part in (top, middle, bottom)
        ]
        chosen = (picked[0] + picked[1] + picked[2]) * pick[T : T + 2 * Q, at].astype(F32)
        one = 1.0 / (base[0:1, at] + jnp.sum(chosen, axis=0, keepdims=True))
        inverse[0, :, at] = jnp.broadcast_to(one, (Q, WIDE))
        inverse[1, :, at] = jnp.broadcast_to(one * base[1:2, at], (Q, WIDE))
        return carry

    lax.fori_loop(0, TILES, diagonal_of, 0)
    loads[10].wait()

    def keep(row, low, values):
        cosines, odds = values
        for k in range(TILES):
            pair = (cosines[0], cosines[8]) if k == 0 else (cosines[k], odds[k])
            for half, value in enumerate(pair):
                for at, part in zip((row, low), split(value)):
                    y[k, pl.ds(at, 2 * Q), T * half : T * half + T] = part

    def first_stage(x):
        e = [x[0]] + [x[n] + x[SECTORS - n] for n in range(1, 8)] + [x[8]]
        return cosine_stage(e), sine_stage([None] + [x[n] - x[SECTORS - n] for n in range(1, 8)])

    def mode_lanes(k):
        return pl.ds(pl.multiple_of(k * WIDE, WIDE), WIDE)

    def forward_rows(start, count, place, offset, extra):
        total = count + (2 if extra else 0)

        def pair(i, carry):
            x = [recv1[n, pl.ds(start + 2 * i, 2)].reshape(2 * Q, T) for n in range(SECTORS)]
            row = pl.multiple_of(offset + 2 * Q * i, 2 * Q)
            keep(row, pl.multiple_of(row + total * Q, 2 * Q), first_stage(x))
            return carry

        lax.fori_loop(0, count // 2, pair, 0)
        if extra:
            x = [jnp.concatenate([precv[n], precv[n]], 0) for n in range(SECTORS)]
            keep(offset + count * Q, offset + count * Q + total * Q, first_stage(x))

        def tile(k, carry):
            out = stacked(y.at[k], pl.ds(offset, 2 * total * Q), total * Q, pl.ds(0, WIDE), (fwd[0, k], fwd[1, k]))
            for begin, amount, target in place:
                modes[pl.ds(REACH + target, amount), :, mode_lanes(k)] = out[begin * Q : (begin + amount) * Q].reshape(amount, Q, WIDE)
            if extra:
                phat[:, mode_lanes(k)] = out[count * Q : count * Q + Q]
            return carry

        lax.fori_loop(0, TILES, tile, 0)

    modes_inner = remote(modes.at[pl.ds(REACH, REACH)], modes.at[pl.ds(REACH + R, REACH)], halo_s.at[10], halo_r.at[10], radial=inner)
    modes_outer = remote(modes.at[pl.ds(R, REACH)], modes.at[pl.ds(0, REACH)], halo_s.at[11], halo_r.at[11], radial=outer)

    forward_all(0).wait_recv()
    forward_all(1).wait_recv()
    forward_rows(0, 2 * EDGE, ((0, EDGE, R - EDGE), (EDGE, EDGE, 0)), 0, False)

    @pl.when(rho > 0)
    def _():
        modes_inner.start()

    @pl.when(rho < RADIALS - 1)
    def _():
        modes_outer.start()

    axial_sum = lam[pl.ds(pl.multiple_of(s * Q, Q), Q), :]
    keep_low = jnp.where(rho > 0, 1.0, 0.0).astype(F32)
    keep_high = jnp.where(rho < RADIALS - 1, 1.0, 0.0).astype(F32)

    def solve_rows(start, stop, groups):
        rows = range(start - REACH, stop + REACH)

        def block(b, carry):
            at = pl.ds(pl.multiple_of(b * T, T), T)
            inv, last, extra = inverse[0, :, at], inverse[1, :, at], phat[:, at]
            low, high = (inv * keep_low, extra * keep_low), (inv * keep_high, extra * keep_high)
            side = {r: low if r < 0 else high if r >= R else (inv, extra) for r in rows}
            c = {r: modes[r + REACH, :, at] + side[r][1] for r in rows}
            x = {r: c[r] * side[r][0] for r in rows}
            for sweep in range(1, SWEEPS):
                x = {
                    r: ((c[r] + axial_sum * x[r]) + (x[r - 1] + x[r + 1])) * (last if sweep == SWEEPS - 1 else side[r][0])
                    for r in range(start - REACH + sweep, stop + REACH - sweep)
                }
            for begin, amount in groups:
                for n in range(0, amount, 2):
                    row = 2 * begin * Q + n * Q
                    for place, part in zip((row, row + amount * Q), split(jnp.concatenate([x[begin + n], x[begin + n + 1]], 0))):
                        x2[place : place + 2 * Q, at] = part
            return carry

        lax.fori_loop(0, NT // T, block, 0)

    def backward_chunk(c):
        start, count = RETURNS[c]

        def tile(k, carry):
            zbuf[k, pl.ds(start * Q, count * Q), :] = stacked(
                x2, pl.ds(2 * start * Q, 2 * count * Q), count * Q, mode_lanes(k), (bwd[0, k], bwd[1, k])
            )
            return carry

        lax.fori_loop(0, TILES, tile, 0)

        def row(r, carry):
            at = pl.ds(pl.multiple_of(r * Q, Q), Q)
            z = [(zbuf[k, at, 0:T], zbuf[k, at, T:WIDE]) for k in range(TILES)]
            even = cosine_stage([z[0][0]] + [z[k][0] for k in range(1, TILES)] + [z[0][1]])
            odd = sine_stage([None] + [z[k][1] for k in range(1, TILES)])
            send2[0, r], send2[8, r] = even[0], even[8]
            for n in range(1, 8):
                send2[n, r] = even[n] + odd[n]
                send2[SECTORS - n, r] = even[n] - odd[n]
            return carry

        lax.fori_loop(start, start + count, row, 0)
        part = pl.ds(start, count)

        def go(i):
            peer = lax.rem(s + i, SECTORS)
            remote(send2.at[peer, part], recv2.at[s, part], b_s.at[c], b_r.at[c], sector=peer).start()

        others(go)
        recv2[s, part] = send2[s, part]

    forward_all(2).wait_recv()
    all_press.wait_recv()
    forward_rows(2 * EDGE, 4, ((0, 4, 4),), 4 * EDGE * Q, True)

    @pl.when(rho > 0)
    def _():
        modes_outer.wait_recv()

    @pl.when(rho == 0)
    def _():
        modes[0:REACH] = jnp.zeros((REACH, Q, NT), F32)

    solve_rows(0, RETURNS[0][1], RETURNS[:1])
    loads[11].wait()
    backward_chunk(0)

    forward_all(3).wait_recv()
    forward_rows(2 * EDGE + 4, 4, ((0, 4, 8),), 4 * EDGE * Q + 12 * Q, False)

    @pl.when(rho < RADIALS - 1)
    def _():
        modes_inner.wait_recv()

    @pl.when(rho == RADIALS - 1)
    def _():
        modes[REACH + R : R + 2 * REACH] = jnp.zeros((REACH, Q, NT), F32)

    solve_rows(RETURNS[0][1], R, RETURNS[1:])
    for c in range(1, len(RETURNS)):
        backward_chunk(c)

    for copy in azimuth_halos + wave_halos + heat_halos + [all_heat, all_wave, all_press] + [forward_all(c) for c in range(len(SENDS))]:
        copy.wait_send()

    @pl.when(rho > 0)
    def _():
        to_inner.wait_send()
        modes_inner.wait_send()

    @pl.when(rho < RADIALS - 1)
    def _():
        to_outer.wait_send()
        modes_outer.wait_send()

    def finish(r, carry):
        lines = recv2[:, r].reshape(NZ, T).T
        press[pl.ds(r, T, stride=R), :] = product(split(lines), sine_pair)
        return carry

    for c, (start, count) in enumerate(RETURNS):
        backward_all(c).wait_recv()
        lax.fori_loop(start, start + count, finish, 0)
    for c in range(len(RETURNS)):
        backward_all(c).wait_send()


def shards(density, swirl, heat_rate, acoustic, mode_impedance, mouth_azimuth, mouth_radius):
    tiles, mode, weight = mode_tables()
    sines, axial_sum = axial_tables()
    impedance = jnp.pad(mode_impedance, (0, 2 * Q * T - mode_impedance.shape[0])).reshape(2 * Q, T)
    pick = np.concatenate([np.arange(T)[:, None] == mode[None, :] % T, np.arange(2 * Q)[:, None] == mode[None, :] // T]).astype(BF16)
    base = np.stack([4.0 + 2.0 - 2.0 * np.cos(2 * np.pi * mode / NT), weight]).astype(np.float32)
    base = np.concatenate([base, np.zeros((6, NT), np.float32)])
    lam = np.repeat(axial_sum[:, None], T, 1).astype(np.float32)
    flat = lambda x: x.reshape(T * R, NZ)
    pinned = lambda x: pltpu.with_memory_space_constraint(jnp.asarray(x), pltpu.HBM)
    vmem, anywhere = pl.BlockSpec(memory_space=pltpu.VMEM), pl.BlockSpec(memory_space=pltpu.HBM)
    dma = pltpu.SemaphoreType.DMA
    fields = [density, swirl, heat_rate]
    dn, press, acn = pl.pallas_call(
        kernel,
        out_shape=(
            jax.ShapeDtypeStruct((T * R, NZ), F32),
            jax.ShapeDtypeStruct((T * R, NZ), F32),
            jax.ShapeDtypeStruct((3, T, NZ), F32),
        ),
        in_specs=[anywhere] * 2 + [vmem] + [anywhere] * 10,
        out_specs=(vmem, vmem, vmem),
        scratch_shapes=[
            pltpu.SMEM((BURNERS,), jnp.int32),
            pltpu.SMEM((BURNERS,), jnp.int32),
            pltpu.VMEM(((T + 2) * R, NZ), F32),
            pltpu.VMEM(((T + 2) * R, NZ), F32),
            pltpu.VMEM((T * R, NZ), F32),
            pltpu.VMEM((R + 2, T, NZ), F32),
            pltpu.VMEM((3, T + 16, NZ), F32),
            pltpu.VMEM((T + 16, NZ), F32),
            pltpu.VMEM((T, NZ), F32),
            pltpu.VMEM((RADIALS, 24, NZ), F32),
            pltpu.VMEM((RADIALS, 3, 8, NZ), F32),
            pltpu.VMEM((SECTORS, Q, T), F32),
            pltpu.VMEM((SECTORS, Q, T), F32),
            pltpu.VMEM((Q, NT), F32),
            pltpu.VMEM((SECTORS, R, Q, T), F32),
            pltpu.VMEM((SECTORS, R, Q, T), F32),
            pltpu.VMEM((SECTORS, R, Q, T), F32),
            pltpu.VMEM((SECTORS, R, Q, T), F32),
            pltpu.VMEM((R + 2 * REACH, Q, NT), F32),
            pltpu.VMEM((TILES, 2 * (R + 2) * Q, WIDE), BF16),
            pltpu.VMEM((2 * R * Q, NT), BF16),
            pltpu.VMEM((TILES, R * Q, WIDE), F32),
            pltpu.VMEM((2, Q, NT), F32),
            pltpu.VMEM((NZ, T), F32),
            pltpu.VMEM((2, NZ, NZ), BF16),
            pltpu.VMEM((T + 2 * Q, NT), BF16),
            pltpu.VMEM((8, NT), F32),
            pltpu.VMEM((2, TILES, WIDE, WIDE), BF16),
            pltpu.VMEM((2, TILES, WIDE, WIDE), BF16),
            dma((12,)),
            dma((12,)),
            dma((12,)),
            dma((3,)),
            dma((3,)),
            dma((len(SENDS),)),
            dma((len(SENDS),)),
            dma((len(RETURNS),)),
            dma((len(RETURNS),)),
        ],
        compiler_params=pltpu.CompilerParams(collective_id=0, has_side_effects=True, vmem_limit_bytes=VMEM_LIMIT),
    )(
        pinned(mouth_azimuth), pinned(mouth_radius), impedance, *[pinned(flat(x)) for x in fields], pinned(acoustic), pinned(lam),
        pinned(halves(sines)), pinned(pick), pinned(base), pinned(halves(tiles)), pinned(halves(tiles.transpose(0, 2, 1))),
    )
    return dn.reshape(T, R, NZ), press.reshape(T, R, NZ), acn


def solution(mesh):
    cells, columns = P("sector", "radial", None), P(None, "sector", None)
    return jax.shard_map(
        shards,
        mesh=mesh,
        in_specs=(cells, cells, cells, columns, P(), P(), P()),
        out_specs=(cells, cells, columns),
        check_vma=False,
    )
```

```python
import math

import jax
import jax.numpy as jnp
import numpy as np
from jax import lax
from jax.experimental import pallas as pl
from jax.experimental.pallas import tpu as pltpu
from jax.sharding import PartitionSpec as P

MOUTH = 8
SWEEPS = 4
SUBSTEPS = 8
REACH = SWEEPS - 1
NT, NR, NZ = 2048, 256, 128
SECTORS, RADIALS = 16, 16
T = NT // SECTORS
R = NR // RADIALS
Q = NZ // SECTORS
TILES = 8
WIDE = 2 * T
BURNERS = 16
EDGE = 4
SENDS = ((0, 1), (1, 3), (4, 4), (8, 4), (12, 4))
RETURNS = ((0, 4), (4, 6), (10, 4), (14, 2))
Y_MIDDLE = 4 * EDGE * Q
EDGE_SENDS, MIDDLE = 3, 4
REST = R - 2 * EDGE - MIDDLE
VMEM_LIMIT = 48 * 2**20

F32, BF16 = jnp.float32, jnp.bfloat16


def halves(table):
    high = table.astype(BF16)
    low = (table - high.astype(np.float64)).astype(BF16)
    return np.stack([high, low])


def mode_tables():
    j = np.arange(T)
    a = np.arange(T)
    tiles = np.zeros((TILES, WIDE, WIDE))
    mode = np.zeros((TILES, WIDE), np.int64)
    for k in range(1, TILES):
        order = SECTORS * a + k
        phase = 2 * np.pi * ((j[:, None] * order[None, :]) % NT) / NT
        tiles[k, :T, :T], tiles[k, :T, T:] = np.cos(phase), np.sin(phase)
        tiles[k, T:, :T], tiles[k, T:, T:] = -np.sin(phase), np.cos(phase)
        mode[k] = np.concatenate([order, order])
    low_cos, low_sin = SECTORS * np.arange(T // 2 + 1), SECTORS * np.arange(1, T // 2)
    mid = SECTORS * np.arange(T // 2) + SECTORS // 2

    def phase_of(order):
        return 2 * np.pi * ((j[:, None] * order[None, :]) % NT) / NT

    tiles[0, :T, :T] = np.concatenate([np.cos(phase_of(low_cos)), np.sin(phase_of(low_sin))], 1)
    tiles[0, T:, T:] = np.concatenate([np.cos(phase_of(mid)), np.sin(phase_of(mid))], 1)
    mode[0] = np.concatenate([low_cos, low_sin, mid, mid])
    mode = np.minimum(mode, NT - mode)
    weight = np.where((mode == 0) | (mode == NT // 2), 1.0, 2.0) / NT
    return tiles, mode.reshape(-1), weight.reshape(-1)


def axial_tables():
    n = np.arange(1, NZ + 1)
    sines = math.sqrt(2.0 / (NZ + 1)) * np.sin(np.pi * ((n[:, None] * n[None, :]) % (2 * (NZ + 1))) / (NZ + 1))
    return sines, 2.0 * np.cos(np.pi * n / (NZ + 1))


C1, C2, C3 = (math.cos(math.pi * n / 8) for n in (1, 2, 3))


def cosine_stage(e):
    f = [e[n] + e[8 - n] for n in range(4)] + [e[4]]
    g = [e[n] - e[8 - n] for n in range(4)]
    outer, inner = f[0] + f[4], f[1] + f[3]
    differ, h = f[0] - f[4], C2 * (f[1] - f[3])
    both = outer + f[2]
    w = C2 * g[2]
    up, down = g[0] + w, g[0] - w
    b, c = C1 * g[1] + C3 * g[3], C3 * g[1] - C1 * g[3]
    return [both + inner, up + b, differ + h, down + c, outer - f[2], down - c, differ - h, up - b, both - inner]


def sine_stage(o):
    u = [None] + [o[n] + o[8 - n] for n in (1, 2, 3)] + [o[4]]
    v = [None] + [o[n] - o[8 - n] for n in (1, 2, 3)]
    h = C2 * (v[1] + v[3])
    w = C2 * u[2]
    up, down = w + u[4], w - u[4]
    b, c = C3 * u[1] + C1 * u[3], C1 * u[1] - C3 * u[3]
    return [None, b + up, h + v[2], c + down, v[1] - v[3], c - down, h - v[2], b - up]


def split(x):
    high = x.astype(BF16)
    return high, (x - high.astype(F32)).astype(BF16)


def product(left, right, dims=((1,), (0,))):
    def one(a, b):
        return lax.dot_general(a, b, (dims, ((), ())), preferred_element_type=F32)

    return one(left[0], right[0]) + (one(left[0], right[1]) + one(left[1], right[0]))


def stacked(ref, rows, half, lanes, right):
    both = lax.dot_general(ref[rows, lanes], right[0], (((1,), (0,)), ((), ())), preferred_element_type=F32)
    high = ref[pl.ds(rows.start, half), lanes]
    return both[:half] + (both[half:] + lax.dot_general(high, right[1], (((1,), (0,)), ((), ())), preferred_element_type=F32))


def kernel(
    azimuth_hbm, radius_hbm, impedance, dens_hbm, swirl_hbm, heat_hbm, ac_hbm, lam_hbm, sines_hbm, pick_hbm, base_hbm, fwd_hbm, bwd_hbm,
    dn, press, acn,
    azimuth, radius, dext, sext, heat, dr, acx, hext, tmask, srcbuf, agbuf, psend, precv, phat,
    send1, recv1, send2, recv2, modes, y, x2, zbuf, inverse, lam, sines, pick, base, fwd, bwd,
    load_sem, halo_s, halo_r, few_s, few_r, f_s, f_r, b_s, b_r,
):
    s, rho = lax.axis_index("sector"), lax.axis_index("radial")
    after, before = lax.rem(s + 1, SECTORS), lax.rem(s + SECTORS - 1, SECTORS)
    inner, outer = lax.rem(rho + RADIALS - 1, RADIALS), lax.rem(rho + 1, RADIALS)
    all_but_one = pl.ds(0, SECTORS - 1)

    def remote(src, dst, send, recv, **where):
        return pltpu.make_async_remote_copy(
            src_ref=src, dst_ref=dst, send_sem=send, recv_sem=recv, device_id=where, device_id_type=pl.DeviceIdType.MESH
        )

    def others(body):
        def step(i, carry):
            body(i)
            return carry

        lax.fori_loop(1, SECTORS, step, 0)

    loads = [
        pltpu.make_async_copy(src, dst, load_sem.at[n])
        for n, (src, dst) in enumerate(
            [
                (dens_hbm, dext.at[pl.ds(R, T * R)]),
                (heat_hbm, heat),
                (swirl_hbm, sext.at[pl.ds(R, T * R)]),
                (azimuth_hbm, azimuth),
                (radius_hbm, radius),
                (sines_hbm, sines),
                (ac_hbm, acx.at[:, pl.ds(8, T)]),
                (lam_hbm, lam),
                (pick_hbm, pick),
                (base_hbm, base),
                (fwd_hbm, fwd),
                (bwd_hbm, bwd),
            ]
        )
    ]
    barrier = pltpu.get_barrier_semaphore()

    def greet(i):
        pl.semaphore_signal(barrier, inc=1, device_id={"sector": lax.rem(s + i, SECTORS)}, device_id_type=pl.DeviceIdType.MESH)
        pl.semaphore_signal(barrier, inc=1, device_id={"radial": lax.rem(rho + i, RADIALS)}, device_id_type=pl.DeviceIdType.MESH)

    others(greet)
    for load in loads[:7]:
        load.start()
    pl.semaphore_wait(barrier, 2 * (SECTORS - 1))

    head, tail = pl.ds(0, R), pl.ds(T * R + R, R)
    azimuth_halos = [
        remote(dens_hbm.at[pl.ds(0, R)], dext.at[tail], halo_s.at[0], halo_r.at[0], sector=before),
        remote(dens_hbm.at[pl.ds(T * R - R, R)], dext.at[head], halo_s.at[1], halo_r.at[1], sector=after),
        remote(swirl_hbm.at[pl.ds(0, R)], sext.at[tail], halo_s.at[2], halo_r.at[2], sector=before),
        remote(swirl_hbm.at[pl.ds(T * R - R, R)], sext.at[head], halo_s.at[3], halo_r.at[3], sector=after),
    ]
    wave_halos = [
        remote(ac_hbm.at[:, pl.ds(0, 8)], acx.at[:, pl.ds(T + 8, 8)], halo_s.at[4], halo_r.at[4], sector=before),
        remote(ac_hbm.at[:, pl.ds(T - 8, 8)], acx.at[:, pl.ds(0, 8)], halo_s.at[5], halo_r.at[5], sector=after),
    ]
    to_inner = remote(dr.at[1], dr.at[R + 1], halo_s.at[6], halo_r.at[6], radial=inner)
    to_outer = remote(dr.at[R], dr.at[0], halo_s.at[7], halo_r.at[7], radial=outer)
    for copy in azimuth_halos:
        copy.start()
    loads[0].wait()
    dr[1] = dext[pl.ds(R, T, stride=R), :]
    dr[R] = dext[pl.ds(2 * R - 1, T, stride=R), :]

    @pl.when(rho > 0)
    def _():
        to_inner.start()

    @pl.when(rho < RADIALS - 1)
    def _():
        to_outer.start()

    for copy in wave_halos:
        copy.start()
    loads[1].wait()

    def heat_row(r, total):
        d = dext[pl.ds(R + r, T, stride=R), :]
        dr[r + 1] = d
        return total + heat[pl.ds(r, T, stride=R), :] * d * d

    ends = heat[pl.ds(0, T, stride=R), :] * dr[1] * dr[1] + heat[pl.ds(R - 1, T, stride=R), :] * dr[R] * dr[R]
    hext[8 : 8 + T, :] = lax.fori_loop(1, R - 1, heat_row, ends) * (1.0 / NR)
    heat_halos = [
        remote(hext.at[pl.ds(8, 8)], hext.at[pl.ds(T + 8, 8)], halo_s.at[8], halo_r.at[8], sector=before),
        remote(hext.at[pl.ds(T, 8)], hext.at[pl.ds(0, 8)], halo_s.at[9], halo_r.at[9], sector=after),
    ]
    for copy in heat_halos:
        copy.start()
    for load in loads[7:]:
        load.start()

    for n in (3, 4, 5, 2):
        loads[n].wait()
    theta = lax.broadcasted_iota(jnp.int32, (T, NZ), 0)
    first = azimuth[s]
    tmask[...] = jnp.where((theta >= first) & (theta < first + MOUTH), 1.0, 0.0).astype(F32)
    lane = lax.broadcasted_iota(jnp.int32, (T, NZ), 1)
    for copy in azimuth_halos:
        copy.wait_recv()

    sine_pair = (sines[0], sines[1])

    def flow_row(i, carry):
        r = lax.rem(i + R - EDGE, R)
        d = dr[r + 1]
        up = dext[pl.ds(2 * R + r, T, stride=R), :]
        down = dext[pl.ds(r, T, stride=R), :]
        axial = jnp.where(lane < NZ - 1, pltpu.roll(d, NZ - 1, 1), 0.0) + jnp.where(lane > 0, pltpu.roll(d, 1, 1), 0.0)
        laplace = (up + down) + (dr[r] + dr[r + 2]) + axial - 6.0 * d
        flux = sext[pl.ds(2 * R + r, T, stride=R), :] * up - sext[pl.ds(r, T, stride=R), :] * down
        where = rho * R + r - radius[s]
        mouth = jnp.where((where >= 0) & (where < MOUTH), 2.5, 0.0).astype(F32)
        change = 0.05 * laplace - 0.5 * flux + (mouth * tmask[...]) * (1.0 - d)
        dn[pl.ds(r, T, stride=R), :] = d + 0.2 * change
        lines = product(sine_pair, split(change), ((1,), (1,)))
        send1[:, i] = lines.reshape(SECTORS, Q, T)
        return carry

    def flow_chunk(c):
        start, count = SENDS[c]
        lax.fori_loop(start, start + count, flow_row, 0)
        part = pl.ds(start, count)

        def go(i):
            peer = lax.rem(s + i, SECTORS)
            remote(send1.at[peer, part], recv1.at[s, part], f_s.at[c], f_r.at[c], sector=peer).start()

        others(go)
        recv1[s, part] = send1[s, part]

    def forward_all(c):
        part = pl.ds(*SENDS[c])
        return remote(send1.at[all_but_one, part], recv1.at[all_but_one, part], f_s.at[c], f_r.at[c], sector=after)

    def backward_all(c):
        part = pl.ds(*RETURNS[c])
        return remote(send2.at[all_but_one, part], recv2.at[all_but_one, part], b_s.at[c], b_r.at[c], sector=after)

    def tile_rows(peer):
        return pl.ds(pl.multiple_of(8 * peer, 8), 24)

    def share_heat(i):
        peer = lax.rem(rho + i, RADIALS)
        remote(hext.at[tile_rows(peer)], srcbuf.at[rho], few_s.at[0], few_r.at[0], radial=peer).start()

    def share_wave(i):
        peer = lax.rem(rho + i, RADIALS)
        remote(agbuf.at[rho], agbuf.at[rho], few_s.at[1], few_r.at[1], radial=peer).start()

    def share_press(i):
        peer = lax.rem(s + i, SECTORS)
        remote(psend.at[peer], precv.at[s], few_s.at[2], few_r.at[2], sector=peer).start()

    all_heat = remote(srcbuf.at[all_but_one], srcbuf.at[all_but_one], few_s.at[0], few_r.at[0], radial=outer)
    all_wave = remote(agbuf.at[all_but_one], agbuf.at[all_but_one], few_s.at[1], few_r.at[1], radial=outer)
    all_press = remote(psend.at[all_but_one], precv.at[all_but_one], few_s.at[2], few_r.at[2], sector=after)

    flow_chunk(0)

    @pl.when(rho > 0)
    def _():
        to_outer.wait_recv()

    @pl.when(rho == 0)
    def _():
        dr[0] = jnp.zeros((T, NZ), F32)

    @pl.when(rho < RADIALS - 1)
    def _():
        to_inner.wait_recv()

    @pl.when(rho == RADIALS - 1)
    def _():
        dr[R + 1] = jnp.zeros((T, NZ), F32)

    for copy in heat_halos + wave_halos:
        copy.wait_recv()
    others(share_heat)
    srcbuf[rho] = hext[tile_rows(rho), :]

    for c in range(1, EDGE_SENDS):
        flow_chunk(c)

    loads[6].wait()
    all_heat.wait_recv()
    source = srcbuf[0]
    for i in range(1, RADIALS):
        source = source + srcbuf[i]
    source = 0.5 * source
    lane24 = lax.broadcasted_iota(jnp.int32, (24, NZ), 1)
    p, u, w = (acx[n, tile_rows(rho), :] for n in range(3))
    for _ in range(SUBSTEPS):
        u = u - 0.5 * (pltpu.roll(p, 23, 0) - p)
        w = w - 0.5 * (jnp.where(lane24 < NZ - 1, pltpu.roll(p, NZ - 1, 1), 0.0) - p)
        along, axial = u - pltpu.roll(u, 1, 0), w - jnp.where(lane24 > 0, pltpu.roll(w, 1, 1), 0.0)
        p = p - 0.5 * (along + axial) + source
    for n, field in enumerate((p, u, w)):
        agbuf[rho, n] = field[8:16]
    others(share_wave)

    flow_chunk(EDGE_SENDS)

    all_wave.wait_recv()
    for n in range(3):
        acn[n] = agbuf[:, n].reshape(T, NZ)
    psend[...] = product(sine_pair, split(0.5 * acn[0]), ((1,), (1,))).reshape(SECTORS, Q, T)
    others(share_press)
    precv[s] = psend[s]

    flow_chunk(EDGE_SENDS + 1)

    for n in (7, 8, 9):
        loads[n].wait()
    whole = impedance[...]
    top = whole.astype(BF16)
    rest = whole - top.astype(F32)
    middle = rest.astype(BF16)
    bottom = (rest - middle.astype(F32)).astype(BF16)

    def diagonal_of(k, carry):
        at = pl.ds(pl.multiple_of(k * WIDE, WIDE), WIDE)
        picked = [
            lax.dot_general(part, pick[0:T, at], (((1,), (0,)), ((), ())), preferred_element_type=F32) for part in (top, middle, bottom)
        ]
        chosen = (picked[0] + picked[1] + picked[2]) * pick[T : T + 2 * Q, at].astype(F32)
        one = 1.0 / (base[0:1, at] + jnp.sum(chosen, axis=0, keepdims=True))
        inverse[0, :, at] = jnp.broadcast_to(one, (Q, WIDE))
        inverse[1, :, at] = jnp.broadcast_to(one * base[1:2, at], (Q, WIDE))
        return carry

    lax.fori_loop(0, TILES, diagonal_of, 0)
    loads[10].wait()

    def keep(row, low, values):
        cosines, odds = values
        for k in range(TILES):
            pair = (cosines[0], cosines[8]) if k == 0 else (cosines[k], odds[k])
            for half, value in enumerate(pair):
                for at, part in zip((row, low), split(value)):
                    y[k, pl.ds(at, 2 * Q), T * half : T * half + T] = part

    def first_stage(x):
        e = [x[0]] + [x[n] + x[SECTORS - n] for n in range(1, 8)] + [x[8]]
        return cosine_stage(e), sine_stage([None] + [x[n] - x[SECTORS - n] for n in range(1, 8)])

    def mode_lanes(k):
        return pl.ds(pl.multiple_of(k * WIDE, WIDE), WIDE)

    def forward_rows(start, count, place, offset, extra):
        total = count + (2 if extra else 0)

        def pair(i, carry):
            x = [recv1[n, pl.ds(start + 2 * i, 2)].reshape(2 * Q, T) for n in range(SECTORS)]
            row = pl.multiple_of(offset + 2 * Q * i, 2 * Q)
            keep(row, pl.multiple_of(row + total * Q, 2 * Q), first_stage(x))
            return carry

        lax.fori_loop(0, count // 2, pair, 0)
        if extra:
            x = [jnp.concatenate([precv[n], precv[n]], 0) for n in range(SECTORS)]
            keep(offset + count * Q, offset + count * Q + total * Q, first_stage(x))

        def tile(k, carry):
            out = stacked(y.at[k], pl.ds(offset, 2 * total * Q), total * Q, pl.ds(0, WIDE), (fwd[0, k], fwd[1, k]))
            for begin, amount, target in place:
                modes[pl.ds(REACH + target, amount), :, mode_lanes(k)] = out[begin * Q : (begin + amount) * Q].reshape(amount, Q, WIDE)
            if extra:
                phat[:, mode_lanes(k)] = out[count * Q : count * Q + Q]
            return carry

        lax.fori_loop(0, TILES, tile, 0, unroll=True)

    modes_inner = remote(modes.at[pl.ds(REACH, REACH)], modes.at[pl.ds(REACH + R, REACH)], halo_s.at[10], halo_r.at[10], radial=inner)
    modes_outer = remote(modes.at[pl.ds(R, REACH)], modes.at[pl.ds(0, REACH)], halo_s.at[11], halo_r.at[11], radial=outer)

    for c in range(EDGE_SENDS):
        forward_all(c).wait_recv()
    forward_rows(0, 2 * EDGE, ((0, EDGE, R - EDGE), (EDGE, EDGE, 0)), 0, False)

    @pl.when(rho > 0)
    def _():
        modes_inner.start()

    @pl.when(rho < RADIALS - 1)
    def _():
        modes_outer.start()

    axial_sum = lam[pl.ds(pl.multiple_of(s * Q, Q), Q), :]
    keep_low = jnp.where(rho > 0, 1.0, 0.0).astype(F32)
    keep_high = jnp.where(rho < RADIALS - 1, 1.0, 0.0).astype(F32)

    def solve_rows(start, stop, groups):
        rows = range(start - REACH, stop + REACH)

        def block(b, carry):
            at = pl.ds(pl.multiple_of(b * T, T), T)
            inv, last, extra = inverse[0, :, at], inverse[1, :, at], phat[:, at]
            low, high = (inv * keep_low, extra * keep_low), (inv * keep_high, extra * keep_high)
            side = {r: low if r < 0 else high if r >= R else (inv, extra) for r in rows}
            c = {r: modes[r + REACH, :, at] + side[r][1] for r in rows}
            x = {r: c[r] * side[r][0] for r in rows}
            for sweep in range(1, SWEEPS):
                x = {
                    r: ((c[r] + axial_sum * x[r]) + (x[r - 1] + x[r + 1])) * (last if sweep == SWEEPS - 1 else side[r][0])
                    for r in range(start - REACH + sweep, stop + REACH - sweep)
                }
            for begin, amount in groups:
                for n in range(0, amount, 2):
                    row = 2 * begin * Q + n * Q
                    for place, part in zip((row, row + amount * Q), split(jnp.concatenate([x[begin + n], x[begin + n + 1]], 0))):
                        x2[place : place + 2 * Q, at] = part
            return carry

        lax.fori_loop(0, NT // T, block, 0)

    def backward_chunk(c):
        start, count = RETURNS[c]

        def tile(k, carry):
            zbuf[k, pl.ds(start * Q, count * Q), :] = stacked(
                x2, pl.ds(2 * start * Q, 2 * count * Q), count * Q, mode_lanes(k), (bwd[0, k], bwd[1, k])
            )
            return carry

        lax.fori_loop(0, TILES, tile, 0, unroll=True)

        def row(r, carry):
            at = pl.ds(pl.multiple_of(r * Q, Q), Q)
            z = [(zbuf[k, at, 0:T], zbuf[k, at, T:WIDE]) for k in range(TILES)]
            even = cosine_stage([z[0][0]] + [z[k][0] for k in range(1, TILES)] + [z[0][1]])
            odd = sine_stage([None] + [z[k][1] for k in range(1, TILES)])
            send2[0, r], send2[8, r] = even[0], even[8]
            for n in range(1, 8):
                send2[n, r] = even[n] + odd[n]
                send2[SECTORS - n, r] = even[n] - odd[n]
            return carry

        lax.fori_loop(start, start + count, row, 0)
        part = pl.ds(start, count)

        def go(i):
            peer = lax.rem(s + i, SECTORS)
            remote(send2.at[peer, part], recv2.at[s, part], b_s.at[c], b_r.at[c], sector=peer).start()

        others(go)
        recv2[s, part] = send2[s, part]

    forward_all(EDGE_SENDS).wait_recv()
    all_press.wait_recv()
    forward_rows(2 * EDGE, MIDDLE, ((0, MIDDLE, EDGE),), Y_MIDDLE, True)

    @pl.when(rho > 0)
    def _():
        modes_outer.wait_recv()

    @pl.when(rho == 0)
    def _():
        modes[0:REACH] = jnp.zeros((REACH, Q, NT), F32)

    solve_rows(0, RETURNS[0][1], RETURNS[:1])
    loads[11].wait()
    backward_chunk(0)

    forward_all(EDGE_SENDS + 1).wait_recv()
    forward_rows(2 * EDGE + MIDDLE, REST, ((0, REST, EDGE + MIDDLE),), Y_MIDDLE + 2 * (MIDDLE + 2) * Q, False)

    @pl.when(rho < RADIALS - 1)
    def _():
        modes_inner.wait_recv()

    @pl.when(rho == RADIALS - 1)
    def _():
        modes[REACH + R : R + 2 * REACH] = jnp.zeros((REACH, Q, NT), F32)

    solve_rows(RETURNS[0][1], R, RETURNS[1:])
    for c in range(1, len(RETURNS)):
        backward_chunk(c)

    for copy in azimuth_halos + wave_halos + heat_halos + [all_heat, all_wave, all_press] + [forward_all(c) for c in range(len(SENDS))]:
        copy.wait_send()

    @pl.when(rho > 0)
    def _():
        to_inner.wait_send()
        modes_inner.wait_send()

    @pl.when(rho < RADIALS - 1)
    def _():
        to_outer.wait_send()
        modes_outer.wait_send()

    def finish(r, carry):
        lines = recv2[:, r].reshape(NZ, T).T
        press[pl.ds(r, T, stride=R), :] = product(split(lines), sine_pair)
        return carry

    for c, (start, count) in enumerate(RETURNS):
        backward_all(c).wait_recv()
        lax.fori_loop(start, start + count, finish, 0)
    for c in range(len(RETURNS)):
        backward_all(c).wait_send()


def deliver(dn, press, acn, dn_hbm, press_hbm, acn_hbm, sem):
    copies = [pltpu.make_async_copy(*pair, sem.at[n]) for n, pair in enumerate(((dn, dn_hbm), (press, press_hbm), (acn, acn_hbm)))]
    for copy in copies:
        copy.start()
    for copy in copies:
        copy.wait()


def shards(density, swirl, heat_rate, acoustic, mode_impedance, mouth_azimuth, mouth_radius):
    tiles, mode, weight = mode_tables()
    sines, axial_sum = axial_tables()
    impedance = jnp.pad(mode_impedance, (0, 2 * Q * T - mode_impedance.shape[0])).reshape(2 * Q, T)
    pick = np.concatenate([np.arange(T)[:, None] == mode[None, :] % T, np.arange(2 * Q)[:, None] == mode[None, :] // T]).astype(BF16)
    base = np.stack([4.0 + 2.0 - 2.0 * np.cos(2 * np.pi * mode / NT), weight]).astype(np.float32)
    base = np.concatenate([base, np.zeros((6, NT), np.float32)])
    lam = np.repeat(axial_sum[:, None], T, 1).astype(np.float32)
    flat = lambda x: x.reshape(T * R, NZ)
    pinned = lambda x: pltpu.with_memory_space_constraint(jnp.asarray(x), pltpu.HBM)
    vmem, anywhere = pl.BlockSpec(memory_space=pltpu.VMEM), pl.BlockSpec(memory_space=pltpu.HBM)
    dma = pltpu.SemaphoreType.DMA
    fields = [density, swirl, heat_rate]
    dn, press, acn = pl.pallas_call(
        kernel,
        out_shape=(
            jax.ShapeDtypeStruct((T * R, NZ), F32),
            jax.ShapeDtypeStruct((T * R, NZ), F32),
            jax.ShapeDtypeStruct((3, T, NZ), F32),
        ),
        in_specs=[anywhere] * 2 + [vmem] + [anywhere] * 10,
        out_specs=(vmem, vmem, vmem),
        scratch_shapes=[
            pltpu.SMEM((BURNERS,), jnp.int32),
            pltpu.SMEM((BURNERS,), jnp.int32),
            pltpu.VMEM(((T + 2) * R, NZ), F32),
            pltpu.VMEM(((T + 2) * R, NZ), F32),
            pltpu.VMEM((T * R, NZ), F32),
            pltpu.VMEM((R + 2, T, NZ), F32),
            pltpu.VMEM((3, T + 16, NZ), F32),
            pltpu.VMEM((T + 16, NZ), F32),
            pltpu.VMEM((T, NZ), F32),
            pltpu.VMEM((RADIALS, 24, NZ), F32),
            pltpu.VMEM((RADIALS, 3, 8, NZ), F32),
            pltpu.VMEM((SECTORS, Q, T), F32),
            pltpu.VMEM((SECTORS, Q, T), F32),
            pltpu.VMEM((Q, NT), F32),
            pltpu.VMEM((SECTORS, R, Q, T), F32),
            pltpu.VMEM((SECTORS, R, Q, T), F32),
            pltpu.VMEM((SECTORS, R, Q, T), F32),
            pltpu.VMEM((SECTORS, R, Q, T), F32),
            pltpu.VMEM((R + 2 * REACH, Q, NT), F32),
            pltpu.VMEM((TILES, 2 * (R + 2) * Q, WIDE), BF16),
            pltpu.VMEM((2 * R * Q, NT), BF16),
            pltpu.VMEM((TILES, R * Q, WIDE), F32),
            pltpu.VMEM((2, Q, NT), F32),
            pltpu.VMEM((NZ, T), F32),
            pltpu.VMEM((2, NZ, NZ), BF16),
            pltpu.VMEM((T + 2 * Q, NT), BF16),
            pltpu.VMEM((8, NT), F32),
            pltpu.VMEM((2, TILES, WIDE, WIDE), BF16),
            pltpu.VMEM((2, TILES, WIDE, WIDE), BF16),
            dma((12,)),
            dma((12,)),
            dma((12,)),
            dma((3,)),
            dma((3,)),
            dma((len(SENDS),)),
            dma((len(SENDS),)),
            dma((len(RETURNS),)),
            dma((len(RETURNS),)),
        ],
        compiler_params=pltpu.CompilerParams(collective_id=0, has_side_effects=True, vmem_limit_bytes=VMEM_LIMIT),
    )(
        pinned(mouth_azimuth), pinned(mouth_radius), impedance, *[pinned(flat(x)) for x in fields], pinned(acoustic), pinned(lam),
        pinned(halves(sines)), pinned(pick), pinned(base), pinned(halves(tiles)), pinned(halves(tiles.transpose(0, 2, 1))),
    )
    results = (dn, press, acn)
    dn, press, acn = pl.pallas_call(
        deliver,
        out_shape=tuple(jax.ShapeDtypeStruct(x.shape, F32) for x in results),
        in_specs=[vmem] * 3,
        out_specs=(anywhere,) * 3,
        scratch_shapes=[dma((3,))],
        compiler_params=pltpu.CompilerParams(vmem_limit_bytes=2**20),
    )(*results)
    return dn.reshape(T, R, NZ), press.reshape(T, R, NZ), acn


def solution(mesh):
    cells, columns = P("sector", "radial", None), P(None, "sector", None)
    return jax.shard_map(
        shards,
        mesh=mesh,
        in_specs=(cells, cells, cells, columns, P(), P(), P()),
        out_specs=(cells, cells, columns),
        check_vma=False,
    )
```

```python
import math

import jax
import jax.numpy as jnp
import numpy as np
from jax import lax
from jax.experimental import pallas as pl
from jax.experimental.pallas import tpu as pltpu
from jax.sharding import PartitionSpec as P

MOUTH = 8
SWEEPS = 4
SUBSTEPS = 8
REACH = SWEEPS - 1
NT, NR, NZ = 2048, 256, 128
SECTORS, RADIALS = 16, 16
T = NT // SECTORS
R = NR // RADIALS
Q = NZ // SECTORS
TILES = 8
WIDE = 2 * T
BURNERS = 16
EDGE = 4
SENDS = ((0, 1), (1, 3), (4, 4), (8, 4), (12, 4))
RETURNS = ((0, 4), (4, 4), (8, 6), (14, 2))
Y_MIDDLE = 4 * EDGE * Q
EDGE_SENDS, MIDDLE = 3, 4
REST = R - 2 * EDGE - MIDDLE
VMEM_LIMIT = 48 * 2**20

F32, BF16 = jnp.float32, jnp.bfloat16


def halves(table):
    high = table.astype(BF16)
    low = (table - high.astype(np.float64)).astype(BF16)
    return np.stack([high, low])


def mode_tables():
    j = np.arange(T)
    a = np.arange(T)
    tiles = np.zeros((TILES, WIDE, WIDE))
    mode = np.zeros((TILES, WIDE), np.int64)
    for k in range(1, TILES):
        order = SECTORS * a + k
        phase = 2 * np.pi * ((j[:, None] * order[None, :]) % NT) / NT
        tiles[k, :T, :T], tiles[k, :T, T:] = np.cos(phase), np.sin(phase)
        tiles[k, T:, :T], tiles[k, T:, T:] = -np.sin(phase), np.cos(phase)
        mode[k] = np.concatenate([order, order])
    low_cos, low_sin = SECTORS * np.arange(T // 2 + 1), SECTORS * np.arange(1, T // 2)
    mid = SECTORS * np.arange(T // 2) + SECTORS // 2

    def phase_of(order):
        return 2 * np.pi * ((j[:, None] * order[None, :]) % NT) / NT

    tiles[0, :T, :T] = np.concatenate([np.cos(phase_of(low_cos)), np.sin(phase_of(low_sin))], 1)
    tiles[0, T:, T:] = np.concatenate([np.cos(phase_of(mid)), np.sin(phase_of(mid))], 1)
    mode[0] = np.concatenate([low_cos, low_sin, mid, mid])
    mode = np.minimum(mode, NT - mode)
    weight = np.where((mode == 0) | (mode == NT // 2), 1.0, 2.0) / NT
    return tiles, mode.reshape(-1), weight.reshape(-1)


def axial_tables():
    n = np.arange(1, NZ + 1)
    sines = math.sqrt(2.0 / (NZ + 1)) * np.sin(np.pi * ((n[:, None] * n[None, :]) % (2 * (NZ + 1))) / (NZ + 1))
    return sines, 2.0 * np.cos(np.pi * n / (NZ + 1))


C1, C2, C3 = (math.cos(math.pi * n / 8) for n in (1, 2, 3))


def cosine_stage(e):
    f = [e[n] + e[8 - n] for n in range(4)] + [e[4]]
    g = [e[n] - e[8 - n] for n in range(4)]
    outer, inner = f[0] + f[4], f[1] + f[3]
    differ, h = f[0] - f[4], C2 * (f[1] - f[3])
    both = outer + f[2]
    w = C2 * g[2]
    up, down = g[0] + w, g[0] - w
    b, c = C1 * g[1] + C3 * g[3], C3 * g[1] - C1 * g[3]
    return [both + inner, up + b, differ + h, down + c, outer - f[2], down - c, differ - h, up - b, both - inner]


def sine_stage(o):
    u = [None] + [o[n] + o[8 - n] for n in (1, 2, 3)] + [o[4]]
    v = [None] + [o[n] - o[8 - n] for n in (1, 2, 3)]
    h = C2 * (v[1] + v[3])
    w = C2 * u[2]
    up, down = w + u[4], w - u[4]
    b, c = C3 * u[1] + C1 * u[3], C1 * u[1] - C3 * u[3]
    return [None, b + up, h + v[2], c + down, v[1] - v[3], c - down, h - v[2], b - up]


def split(x):
    high = x.astype(BF16)
    return high, (x - high.astype(F32)).astype(BF16)


def product(left, right, dims=((1,), (0,))):
    def one(a, b):
        return lax.dot_general(a, b, (dims, ((), ())), preferred_element_type=F32)

    return one(left[0], right[0]) + (one(left[0], right[1]) + one(left[1], right[0]))


def stacked(ref, rows, half, lanes, right):
    both = lax.dot_general(ref[rows, lanes], right[0], (((1,), (0,)), ((), ())), preferred_element_type=F32)
    high = ref[pl.ds(rows.start, half), lanes]
    return both[:half] + (both[half:] + lax.dot_general(high, right[1], (((1,), (0,)), ((), ())), preferred_element_type=F32))


def kernel(
    azimuth_hbm, radius_hbm, impedance_hbm, dens_hbm, swirl_hbm, heat_hbm, ac_hbm, lam_hbm, sines_hbm, pick_hbm, base_hbm, fwd_hbm, bwd_hbm,
    dn, press, acn,
    azimuth, radius, impedance, topmost, dext, sext, heat, dr, acx, hext, tmask, srcbuf, agbuf, psend, precv, phat,
    send1, recv1, send2, recv2, modes, y, x2, zbuf, inverse, lam, sines, pick, base, fwd, bwd,
    load_sem, halo_s, halo_r, few_s, few_r, f_s, f_r, b_s, b_r,
):
    s, rho = lax.axis_index("sector"), lax.axis_index("radial")
    after, before = lax.rem(s + 1, SECTORS), lax.rem(s + SECTORS - 1, SECTORS)
    inner, outer = lax.rem(rho + RADIALS - 1, RADIALS), lax.rem(rho + 1, RADIALS)
    all_but_one = pl.ds(0, SECTORS - 1)

    def remote(src, dst, send, recv, **where):
        return pltpu.make_async_remote_copy(
            src_ref=src, dst_ref=dst, send_sem=send, recv_sem=recv, device_id=where, device_id_type=pl.DeviceIdType.MESH
        )

    def others(body):
        def step(i, carry):
            body(i)
            return carry

        lax.fori_loop(1, SECTORS, step, 0)

    low, inside, high = pl.ds(0, R), pl.ds(R, (T - 2) * R), pl.ds(T * R - R, R)
    loads = [
        pltpu.make_async_copy(src, dst, load_sem.at[n])
        for n, (src, dst) in enumerate(
            [
                (dens_hbm.at[inside], dext.at[pl.ds(2 * R, (T - 2) * R)]),
                (heat_hbm, heat),
                (swirl_hbm.at[inside], sext.at[pl.ds(2 * R, (T - 2) * R)]),
                (azimuth_hbm, azimuth),
                (radius_hbm, radius),
                (sines_hbm, sines),
                (ac_hbm, acx.at[:, pl.ds(8, T)]),
                (lam_hbm, lam),
                (pick_hbm, pick),
                (base_hbm, base),
                (fwd_hbm, fwd),
                (bwd_hbm, bwd),
                (impedance_hbm, impedance),
                (impedance_hbm, topmost),
                (dens_hbm.at[low], dext.at[pl.ds(R, R)]),
                (dens_hbm.at[high], dext.at[pl.ds(T * R, R)]),
                (swirl_hbm.at[low], sext.at[pl.ds(R, R)]),
                (swirl_hbm.at[high], sext.at[pl.ds(T * R, R)]),
            ]
        )
    ]
    barrier = pltpu.get_barrier_semaphore()

    def greet(i):
        pl.semaphore_signal(barrier, inc=1, device_id={"sector": lax.rem(s + i, SECTORS)}, device_id_type=pl.DeviceIdType.MESH)
        pl.semaphore_signal(barrier, inc=1, device_id={"radial": lax.rem(rho + i, RADIALS)}, device_id_type=pl.DeviceIdType.MESH)

    others(greet)
    for load in loads[14:] + loads[:7]:
        load.start()
    pl.semaphore_wait(barrier, 2 * (SECTORS - 1))

    head, tail = pl.ds(0, R), pl.ds(T * R + R, R)
    azimuth_halos = [
        remote(dext.at[pl.ds(R, R)], dext.at[tail], halo_s.at[0], halo_r.at[0], sector=before),
        remote(dext.at[pl.ds(T * R, R)], dext.at[head], halo_s.at[1], halo_r.at[1], sector=after),
        remote(sext.at[pl.ds(R, R)], sext.at[tail], halo_s.at[2], halo_r.at[2], sector=before),
        remote(sext.at[pl.ds(T * R, R)], sext.at[head], halo_s.at[3], halo_r.at[3], sector=after),
    ]
    wave_halos = [
        remote(ac_hbm.at[:, pl.ds(0, 8)], acx.at[:, pl.ds(T + 8, 8)], halo_s.at[4], halo_r.at[4], sector=before),
        remote(ac_hbm.at[:, pl.ds(T - 8, 8)], acx.at[:, pl.ds(0, 8)], halo_s.at[5], halo_r.at[5], sector=after),
    ]
    to_inner = remote(dr.at[1], dr.at[R + 1], halo_s.at[6], halo_r.at[6], radial=inner)
    to_outer = remote(dr.at[R], dr.at[0], halo_s.at[7], halo_r.at[7], radial=outer)
    for load in loads[14:]:
        load.wait()
    for copy in azimuth_halos:
        copy.start()
    loads[0].wait()
    dr[1] = dext[pl.ds(R, T, stride=R), :]
    dr[R] = dext[pl.ds(2 * R - 1, T, stride=R), :]

    @pl.when(rho > 0)
    def _():
        to_inner.start()

    @pl.when(rho < RADIALS - 1)
    def _():
        to_outer.start()

    for copy in wave_halos:
        copy.start()
    loads[1].wait()

    def heat_row(r, total):
        d = dext[pl.ds(R + r, T, stride=R), :]
        dr[r + 1] = d
        return total + heat[pl.ds(r, T, stride=R), :] * d * d

    ends = heat[pl.ds(0, T, stride=R), :] * dr[1] * dr[1] + heat[pl.ds(R - 1, T, stride=R), :] * dr[R] * dr[R]
    hext[8 : 8 + T, :] = lax.fori_loop(1, R - 1, heat_row, ends) * (1.0 / NR)
    heat_halos = [
        remote(hext.at[pl.ds(8, 8)], hext.at[pl.ds(T + 8, 8)], halo_s.at[8], halo_r.at[8], sector=before),
        remote(hext.at[pl.ds(T, 8)], hext.at[pl.ds(0, 8)], halo_s.at[9], halo_r.at[9], sector=after),
    ]
    for copy in heat_halos:
        copy.start()
    for load in loads[7:14]:
        load.start()

    for n in (3, 4, 5, 2):
        loads[n].wait()
    theta = lax.broadcasted_iota(jnp.int32, (T, NZ), 0)
    first = azimuth[s]
    tmask[...] = jnp.where((theta >= first) & (theta < first + MOUTH), 1.0, 0.0).astype(F32)
    lane = lax.broadcasted_iota(jnp.int32, (T, NZ), 1)
    for copy in azimuth_halos:
        copy.wait_recv()

    sine_pair = (sines[0], sines[1])

    def flow_row(i, carry):
        r = lax.rem(i + R - EDGE, R)
        d = dr[r + 1]
        up = dext[pl.ds(2 * R + r, T, stride=R), :]
        down = dext[pl.ds(r, T, stride=R), :]
        axial = jnp.where(lane < NZ - 1, pltpu.roll(d, NZ - 1, 1), 0.0) + jnp.where(lane > 0, pltpu.roll(d, 1, 1), 0.0)
        laplace = (up + down) + (dr[r] + dr[r + 2]) + axial - 6.0 * d
        flux = sext[pl.ds(2 * R + r, T, stride=R), :] * up - sext[pl.ds(r, T, stride=R), :] * down
        where = rho * R + r - radius[s]
        mouth = jnp.where((where >= 0) & (where < MOUTH), 2.5, 0.0).astype(F32)
        change = 0.05 * laplace - 0.5 * flux + (mouth * tmask[...]) * (1.0 - d)
        dn[pl.ds(r, T, stride=R), :] = d + 0.2 * change
        lines = product(sine_pair, split(change), ((1,), (1,)))
        send1[:, i] = lines.reshape(SECTORS, Q, T)
        return carry

    def flow_chunk(c):
        start, count = SENDS[c]
        lax.fori_loop(start, start + count, flow_row, 0)
        part = pl.ds(start, count)

        def go(i):
            peer = lax.rem(s + i, SECTORS)
            remote(send1.at[peer, part], recv1.at[s, part], f_s.at[c], f_r.at[c], sector=peer).start()

        others(go)
        recv1[s, part] = send1[s, part]

    def forward_all(c):
        part = pl.ds(*SENDS[c])
        return remote(send1.at[all_but_one, part], recv1.at[all_but_one, part], f_s.at[c], f_r.at[c], sector=after)

    def backward_all(c):
        part = pl.ds(*RETURNS[c])
        return remote(send2.at[all_but_one, part], recv2.at[all_but_one, part], b_s.at[c], b_r.at[c], sector=after)

    def tile_rows(peer):
        return pl.ds(pl.multiple_of(8 * peer, 8), 24)

    def share_heat(i):
        peer = lax.rem(rho + i, RADIALS)
        remote(hext.at[tile_rows(peer)], srcbuf.at[rho], few_s.at[0], few_r.at[0], radial=peer).start()

    def share_wave(i):
        peer = lax.rem(rho + i, RADIALS)
        remote(agbuf.at[rho], agbuf.at[rho], few_s.at[1], few_r.at[1], radial=peer).start()

    def share_press(i):
        peer = lax.rem(s + i, SECTORS)
        remote(psend.at[peer], precv.at[s], few_s.at[2], few_r.at[2], sector=peer).start()

    all_heat = remote(srcbuf.at[all_but_one], srcbuf.at[all_but_one], few_s.at[0], few_r.at[0], radial=outer)
    all_wave = remote(agbuf.at[all_but_one], agbuf.at[all_but_one], few_s.at[1], few_r.at[1], radial=outer)
    all_press = remote(psend.at[all_but_one], precv.at[all_but_one], few_s.at[2], few_r.at[2], sector=after)

    flow_chunk(0)

    @pl.when(rho > 0)
    def _():
        to_outer.wait_recv()

    @pl.when(rho == 0)
    def _():
        dr[0] = jnp.zeros((T, NZ), F32)

    @pl.when(rho < RADIALS - 1)
    def _():
        to_inner.wait_recv()

    @pl.when(rho == RADIALS - 1)
    def _():
        dr[R + 1] = jnp.zeros((T, NZ), F32)

    for copy in heat_halos + wave_halos:
        copy.wait_recv()
    others(share_heat)
    srcbuf[rho] = hext[tile_rows(rho), :]

    for c in range(1, EDGE_SENDS):
        flow_chunk(c)

    loads[6].wait()
    all_heat.wait_recv()
    source = srcbuf[0]
    for i in range(1, RADIALS):
        source = source + srcbuf[i]
    source = 0.5 * source
    lane24 = lax.broadcasted_iota(jnp.int32, (24, NZ), 1)
    p, u, w = (acx[n, tile_rows(rho), :] for n in range(3))
    for _ in range(SUBSTEPS):
        u = u - 0.5 * (pltpu.roll(p, 23, 0) - p)
        w = w - 0.5 * (jnp.where(lane24 < NZ - 1, pltpu.roll(p, NZ - 1, 1), 0.0) - p)
        along, axial = u - pltpu.roll(u, 1, 0), w - jnp.where(lane24 > 0, pltpu.roll(w, 1, 1), 0.0)
        p = p - 0.5 * (along + axial) + source
    for n, field in enumerate((p, u, w)):
        agbuf[rho, n] = field[8:16]
    others(share_wave)

    flow_chunk(EDGE_SENDS)

    all_wave.wait_recv()
    for n in range(3):
        acn[n] = agbuf[:, n].reshape(T, NZ)
    psend[...] = product(sine_pair, split(0.5 * acn[0]), ((1,), (1,))).reshape(SECTORS, Q, T)
    others(share_press)
    precv[s] = psend[s]

    flow_chunk(EDGE_SENDS + 1)

    for n in (7, 8, 9, 12, 13):
        loads[n].wait()
    whole = jnp.concatenate([impedance[0 : NT // 2].reshape(Q, T), jnp.full((Q, T), topmost[NT // 2], F32)], 0)
    top = whole.astype(BF16)
    rest = whole - top.astype(F32)
    middle = rest.astype(BF16)
    bottom = (rest - middle.astype(F32)).astype(BF16)

    def diagonal_of(k, carry):
        at = pl.ds(pl.multiple_of(k * WIDE, WIDE), WIDE)
        picked = [
            lax.dot_general(part, pick[0:T, at], (((1,), (0,)), ((), ())), preferred_element_type=F32) for part in (top, middle, bottom)
        ]
        chosen = (picked[0] + picked[1] + picked[2]) * pick[T : T + 2 * Q, at].astype(F32)
        one = 1.0 / (base[0:1, at] + jnp.sum(chosen, axis=0, keepdims=True))
        inverse[0, :, at] = jnp.broadcast_to(one, (Q, WIDE))
        inverse[1, :, at] = jnp.broadcast_to(one * base[1:2, at], (Q, WIDE))
        return carry

    lax.fori_loop(0, TILES, diagonal_of, 0)
    loads[10].wait()

    def keep(row, low, values):
        cosines, odds = values
        for k in range(TILES):
            pair = (cosines[0], cosines[8]) if k == 0 else (cosines[k], odds[k])
            for half, value in enumerate(pair):
                for at, part in zip((row, low), split(value)):
                    y[k, pl.ds(at, 2 * Q), T * half : T * half + T] = part

    def first_stage(x):
        e = [x[0]] + [x[n] + x[SECTORS - n] for n in range(1, 8)] + [x[8]]
        return cosine_stage(e), sine_stage([None] + [x[n] - x[SECTORS - n] for n in range(1, 8)])

    def mode_lanes(k):
        return pl.ds(pl.multiple_of(k * WIDE, WIDE), WIDE)

    def forward_rows(start, count, place, offset, extra):
        total = count + (2 if extra else 0)

        def pair(i, carry):
            x = [recv1[n, pl.ds(start + 2 * i, 2)].reshape(2 * Q, T) for n in range(SECTORS)]
            row = pl.multiple_of(offset + 2 * Q * i, 2 * Q)
            keep(row, pl.multiple_of(row + total * Q, 2 * Q), first_stage(x))
            return carry

        lax.fori_loop(0, count // 2, pair, 0)
        if extra:
            x = [jnp.concatenate([precv[n], precv[n]], 0) for n in range(SECTORS)]
            keep(offset + count * Q, offset + count * Q + total * Q, first_stage(x))

        def tile(k, carry):
            out = stacked(y.at[k], pl.ds(offset, 2 * total * Q), total * Q, pl.ds(0, WIDE), (fwd[0, k], fwd[1, k]))
            for begin, amount, target in place:
                modes[pl.ds(REACH + target, amount), :, mode_lanes(k)] = out[begin * Q : (begin + amount) * Q].reshape(amount, Q, WIDE)
            if extra:
                phat[:, mode_lanes(k)] = out[count * Q : count * Q + Q]
            return carry

        lax.fori_loop(0, TILES, tile, 0, unroll=True)

    modes_inner = remote(modes.at[pl.ds(REACH, REACH)], modes.at[pl.ds(REACH + R, REACH)], halo_s.at[10], halo_r.at[10], radial=inner)
    modes_outer = remote(modes.at[pl.ds(R, REACH)], modes.at[pl.ds(0, REACH)], halo_s.at[11], halo_r.at[11], radial=outer)

    for c in range(EDGE_SENDS):
        forward_all(c).wait_recv()
    forward_rows(0, 2 * EDGE, ((0, EDGE, R - EDGE), (EDGE, EDGE, 0)), 0, False)

    @pl.when(rho > 0)
    def _():
        modes_inner.start()

    @pl.when(rho < RADIALS - 1)
    def _():
        modes_outer.start()

    axial_sum = lam[pl.ds(pl.multiple_of(s * Q, Q), Q), :]
    keep_low = jnp.where(rho > 0, 1.0, 0.0).astype(F32)
    keep_high = jnp.where(rho < RADIALS - 1, 1.0, 0.0).astype(F32)

    def solve_rows(start, stop, groups):
        rows = range(start - REACH, stop + REACH)

        def block(b, carry):
            at = pl.ds(pl.multiple_of(b * T, T), T)
            inv, last, extra = inverse[0, :, at], inverse[1, :, at], phat[:, at]
            low, high = (inv * keep_low, extra * keep_low), (inv * keep_high, extra * keep_high)
            side = {r: low if r < 0 else high if r >= R else (inv, extra) for r in rows}
            c = {r: modes[r + REACH, :, at] + side[r][1] for r in rows}
            x = {r: c[r] * side[r][0] for r in rows}
            for sweep in range(1, SWEEPS):
                x = {
                    r: ((c[r] + axial_sum * x[r]) + (x[r - 1] + x[r + 1])) * (last if sweep == SWEEPS - 1 else side[r][0])
                    for r in range(start - REACH + sweep, stop + REACH - sweep)
                }
            for begin, amount in groups:
                for n in range(0, amount, 2):
                    row = 2 * begin * Q + n * Q
                    for place, part in zip((row, row + amount * Q), split(jnp.concatenate([x[begin + n], x[begin + n + 1]], 0))):
                        x2[place : place + 2 * Q, at] = part
            return carry

        lax.fori_loop(0, NT // T, block, 0)

    def backward_chunk(c):
        start, count = RETURNS[c]

        def tile(k, carry):
            zbuf[k, pl.ds(start * Q, count * Q), :] = stacked(
                x2, pl.ds(2 * start * Q, 2 * count * Q), count * Q, mode_lanes(k), (bwd[0, k], bwd[1, k])
            )
            return carry

        lax.fori_loop(0, TILES, tile, 0, unroll=True)

        def row(r, carry):
            at = pl.ds(pl.multiple_of(r * Q, Q), Q)
            z = [(zbuf[k, at, 0:T], zbuf[k, at, T:WIDE]) for k in range(TILES)]
            even = cosine_stage([z[0][0]] + [z[k][0] for k in range(1, TILES)] + [z[0][1]])
            odd = sine_stage([None] + [z[k][1] for k in range(1, TILES)])
            send2[0, r], send2[8, r] = even[0], even[8]
            for n in range(1, 8):
                send2[n, r] = even[n] + odd[n]
                send2[SECTORS - n, r] = even[n] - odd[n]
            return carry

        lax.fori_loop(start, start + count, row, 0)
        part = pl.ds(start, count)

        def go(i):
            peer = lax.rem(s + i, SECTORS)
            remote(send2.at[peer, part], recv2.at[s, part], b_s.at[c], b_r.at[c], sector=peer).start()

        others(go)
        recv2[s, part] = send2[s, part]

    forward_all(EDGE_SENDS).wait_recv()
    all_press.wait_recv()
    forward_rows(2 * EDGE, MIDDLE, ((0, MIDDLE, EDGE),), Y_MIDDLE, True)

    @pl.when(rho > 0)
    def _():
        modes_outer.wait_recv()

    @pl.when(rho == 0)
    def _():
        modes[0:REACH] = jnp.zeros((REACH, Q, NT), F32)

    solve_rows(0, RETURNS[0][1], RETURNS[:1])
    loads[11].wait()
    backward_chunk(0)

    forward_all(EDGE_SENDS + 1).wait_recv()
    forward_rows(2 * EDGE + MIDDLE, REST, ((0, REST, EDGE + MIDDLE),), Y_MIDDLE + 2 * (MIDDLE + 2) * Q, False)

    @pl.when(rho < RADIALS - 1)
    def _():
        modes_inner.wait_recv()

    @pl.when(rho == RADIALS - 1)
    def _():
        modes[REACH + R : R + 2 * REACH] = jnp.zeros((REACH, Q, NT), F32)

    for c in range(1, len(RETURNS)):
        start, count = RETURNS[c]
        solve_rows(start, start + count, RETURNS[c : c + 1])
        backward_chunk(c)

    for copy in azimuth_halos + wave_halos + heat_halos + [all_heat, all_wave, all_press] + [forward_all(c) for c in range(len(SENDS))]:
        copy.wait_send()

    @pl.when(rho > 0)
    def _():
        to_inner.wait_send()
        modes_inner.wait_send()

    @pl.when(rho < RADIALS - 1)
    def _():
        to_outer.wait_send()
        modes_outer.wait_send()

    def finish(r, carry):
        lines = recv2[:, r].reshape(NZ, T).T
        press[pl.ds(r, T, stride=R), :] = product(split(lines), sine_pair)
        return carry

    for c, (start, count) in enumerate(RETURNS):
        backward_all(c).wait_recv()
        lax.fori_loop(start, start + count, finish, 0, unroll=2)
    for c in range(len(RETURNS)):
        backward_all(c).wait_send()


def deliver(dn, press, acn, dn_hbm, press_hbm, acn_hbm, sem):
    copies = [pltpu.make_async_copy(*pair, sem.at[n]) for n, pair in enumerate(((dn, dn_hbm), (press, press_hbm), (acn, acn_hbm)))]
    for copy in copies:
        copy.start()
    for copy in copies:
        copy.wait()


def shards(density, swirl, heat_rate, acoustic, mode_impedance, mouth_azimuth, mouth_radius):
    tiles, mode, weight = mode_tables()
    sines, axial_sum = axial_tables()
    pick = np.concatenate([np.arange(T)[:, None] == mode[None, :] % T, np.arange(2 * Q)[:, None] == mode[None, :] // T]).astype(BF16)
    base = np.stack([4.0 + 2.0 - 2.0 * np.cos(2 * np.pi * mode / NT), weight]).astype(np.float32)
    base = np.concatenate([base, np.zeros((6, NT), np.float32)])
    lam = np.repeat(axial_sum[:, None], T, 1).astype(np.float32)
    flat = lambda x: x.reshape(T * R, NZ)
    pinned = lambda x: pltpu.with_memory_space_constraint(jnp.asarray(x), pltpu.HBM)
    vmem, anywhere = pl.BlockSpec(memory_space=pltpu.VMEM), pl.BlockSpec(memory_space=pltpu.HBM)
    dma = pltpu.SemaphoreType.DMA
    fields = [density, swirl, heat_rate]
    dn, press, acn = pl.pallas_call(
        kernel,
        out_shape=(
            jax.ShapeDtypeStruct((T * R, NZ), F32),
            jax.ShapeDtypeStruct((T * R, NZ), F32),
            jax.ShapeDtypeStruct((3, T, NZ), F32),
        ),
        in_specs=[anywhere] * 13,
        out_specs=(vmem, vmem, vmem),
        scratch_shapes=[
            pltpu.SMEM((BURNERS,), jnp.int32),
            pltpu.SMEM((BURNERS,), jnp.int32),
            pltpu.VMEM((NT // 2 + 1,), F32),
            pltpu.SMEM((NT // 2 + 1,), F32),
            pltpu.VMEM(((T + 2) * R, NZ), F32),
            pltpu.VMEM(((T + 2) * R, NZ), F32),
            pltpu.VMEM((T * R, NZ), F32),
            pltpu.VMEM((R + 2, T, NZ), F32),
            pltpu.VMEM((3, T + 16, NZ), F32),
            pltpu.VMEM((T + 16, NZ), F32),
            pltpu.VMEM((T, NZ), F32),
            pltpu.VMEM((RADIALS, 24, NZ), F32),
            pltpu.VMEM((RADIALS, 3, 8, NZ), F32),
            pltpu.VMEM((SECTORS, Q, T), F32),
            pltpu.VMEM((SECTORS, Q, T), F32),
            pltpu.VMEM((Q, NT), F32),
            pltpu.VMEM((SECTORS, R, Q, T), F32),
            pltpu.VMEM((SECTORS, R, Q, T), F32),
            pltpu.VMEM((SECTORS, R, Q, T), F32),
            pltpu.VMEM((SECTORS, R, Q, T), F32),
            pltpu.VMEM((R + 2 * REACH, Q, NT), F32),
            pltpu.VMEM((TILES, 2 * (R + 2) * Q, WIDE), BF16),
            pltpu.VMEM((2 * R * Q, NT), BF16),
            pltpu.VMEM((TILES, R * Q, WIDE), F32),
            pltpu.VMEM((2, Q, NT), F32),
            pltpu.VMEM((NZ, T), F32),
            pltpu.VMEM((2, NZ, NZ), BF16),
            pltpu.VMEM((T + 2 * Q, NT), BF16),
            pltpu.VMEM((8, NT), F32),
            pltpu.VMEM((2, TILES, WIDE, WIDE), BF16),
            pltpu.VMEM((2, TILES, WIDE, WIDE), BF16),
            dma((18,)),
            dma((12,)),
            dma((12,)),
            dma((3,)),
            dma((3,)),
            dma((len(SENDS),)),
            dma((len(SENDS),)),
            dma((len(RETURNS),)),
            dma((len(RETURNS),)),
        ],
        compiler_params=pltpu.CompilerParams(collective_id=0, has_side_effects=True, vmem_limit_bytes=VMEM_LIMIT),
    )(
        pinned(mouth_azimuth), pinned(mouth_radius), pinned(mode_impedance), *[pinned(flat(x)) for x in fields], pinned(acoustic), pinned(lam),
        pinned(halves(sines)), pinned(pick), pinned(base), pinned(halves(tiles)), pinned(halves(tiles.transpose(0, 2, 1))),
    )
    results = (dn, press, acn)
    dn, press, acn = pl.pallas_call(
        deliver,
        out_shape=tuple(jax.ShapeDtypeStruct(x.shape, F32) for x in results),
        in_specs=[vmem] * 3,
        out_specs=(anywhere,) * 3,
        scratch_shapes=[dma((3,))],
        compiler_params=pltpu.CompilerParams(vmem_limit_bytes=2**20),
    )(*results)
    return dn.reshape(T, R, NZ), press.reshape(T, R, NZ), acn


def solution(mesh):
    cells, columns = P("sector", "radial", None), P(None, "sector", None)
    return jax.shard_map(
        shards,
        mesh=mesh,
        in_specs=(cells, cells, cells, columns, P(), P(), P()),
        out_specs=(cells, cells, columns),
        check_vma=False,
    )
```

```python
import math

import jax
import jax.numpy as jnp
import numpy as np
from jax import lax
from jax.experimental import pallas as pl
from jax.experimental.pallas import tpu as pltpu
from jax.sharding import PartitionSpec as P

MOUTH = 8
SWEEPS = 4
SUBSTEPS = 8
REACH = SWEEPS - 1
NT, NR, NZ = 2048, 256, 128
SECTORS, RADIALS = 16, 16
T = NT // SECTORS
R = NR // RADIALS
Q = NZ // SECTORS
TILES = 8
WIDE = 2 * T
BURNERS = 16
EDGE = 4
SENDS = ((0, 1), (1, 3), (4, 4), (8, 4), (12, 4))
RETURNS = ((0, 4), (4, 4), (8, 6), (14, 2))
Y_MIDDLE = 4 * EDGE * Q
EDGE_SENDS, MIDDLE = 3, 4
REST = R - 2 * EDGE - MIDDLE
VMEM_LIMIT = 48 * 2**20

F32, BF16 = jnp.float32, jnp.bfloat16


def halves(table):
    high = table.astype(BF16)
    low = (table - high.astype(np.float64)).astype(BF16)
    return np.stack([high, low])


def mode_tables():
    j = np.arange(T)
    a = np.arange(T)
    tiles = np.zeros((TILES, WIDE, WIDE))
    mode = np.zeros((TILES, WIDE), np.int64)
    for k in range(1, TILES):
        order = SECTORS * a + k
        phase = 2 * np.pi * ((j[:, None] * order[None, :]) % NT) / NT
        tiles[k, :T, :T], tiles[k, :T, T:] = np.cos(phase), np.sin(phase)
        tiles[k, T:, :T], tiles[k, T:, T:] = -np.sin(phase), np.cos(phase)
        mode[k] = np.concatenate([order, order])
    low_cos, low_sin = SECTORS * np.arange(T // 2 + 1), SECTORS * np.arange(1, T // 2)
    mid = SECTORS * np.arange(T // 2) + SECTORS // 2

    def phase_of(order):
        return 2 * np.pi * ((j[:, None] * order[None, :]) % NT) / NT

    tiles[0, :T, :T] = np.concatenate([np.cos(phase_of(low_cos)), np.sin(phase_of(low_sin))], 1)
    tiles[0, T:, T:] = np.concatenate([np.cos(phase_of(mid)), np.sin(phase_of(mid))], 1)
    mode[0] = np.concatenate([low_cos, low_sin, mid, mid])
    mode = np.minimum(mode, NT - mode)
    weight = np.where((mode == 0) | (mode == NT // 2), 1.0, 2.0) / NT
    return tiles, mode.reshape(-1), weight.reshape(-1)


def axial_tables():
    n = np.arange(1, NZ + 1)
    sines = math.sqrt(2.0 / (NZ + 1)) * np.sin(np.pi * ((n[:, None] * n[None, :]) % (2 * (NZ + 1))) / (NZ + 1))
    return sines, 2.0 * np.cos(np.pi * n / (NZ + 1))


C1, C2, C3 = (math.cos(math.pi * n / 8) for n in (1, 2, 3))


def cosine_stage(e):
    f = [e[n] + e[8 - n] for n in range(4)] + [e[4]]
    g = [e[n] - e[8 - n] for n in range(4)]
    outer, inner = f[0] + f[4], f[1] + f[3]
    differ, h = f[0] - f[4], C2 * (f[1] - f[3])
    both = outer + f[2]
    w = C2 * g[2]
    up, down = g[0] + w, g[0] - w
    b, c = C1 * g[1] + C3 * g[3], C3 * g[1] - C1 * g[3]
    return [both + inner, up + b, differ + h, down + c, outer - f[2], down - c, differ - h, up - b, both - inner]


def sine_stage(o):
    u = [None] + [o[n] + o[8 - n] for n in (1, 2, 3)] + [o[4]]
    v = [None] + [o[n] - o[8 - n] for n in (1, 2, 3)]
    h = C2 * (v[1] + v[3])
    w = C2 * u[2]
    up, down = w + u[4], w - u[4]
    b, c = C3 * u[1] + C1 * u[3], C1 * u[1] - C3 * u[3]
    return [None, b + up, h + v[2], c + down, v[1] - v[3], c - down, h - v[2], b - up]


def split(x):
    high = x.astype(BF16)
    return high, (x - high.astype(F32)).astype(BF16)


def product(left, right, dims=((1,), (0,))):
    def one(a, b):
        return lax.dot_general(a, b, (dims, ((), ())), preferred_element_type=F32)

    return one(left[0], right[0]) + (one(left[0], right[1]) + one(left[1], right[0]))


def stacked(ref, rows, half, lanes, right):
    both = lax.dot_general(ref[rows, lanes], right[0], (((1,), (0,)), ((), ())), preferred_element_type=F32)
    high = ref[pl.ds(rows.start, half), lanes]
    return both[:half] + (both[half:] + lax.dot_general(high, right[1], (((1,), (0,)), ((), ())), preferred_element_type=F32))


def kernel(
    azimuth_hbm, radius_hbm, impedance_hbm, dens_hbm, swirl_hbm, heat_hbm, ac_hbm, lam_hbm, sines_hbm, pick_hbm, base_hbm, fwd_hbm, bwd_hbm,
    dn, press, acn,
    azimuth, radius, impedance, topmost, dext, sext, heat, dr, acx, hext, tmask, srcbuf, agbuf, psend, precv, phat,
    send1, recv1, send2, recv2, modes, y, x2, zbuf, inverse, lam, sines, pick, base, fwd, bwd,
    load_sem, halo_s, halo_r, few_s, few_r, f_s, f_r, b_s, b_r,
):
    s, rho = lax.axis_index("sector"), lax.axis_index("radial")
    after, before = lax.rem(s + 1, SECTORS), lax.rem(s + SECTORS - 1, SECTORS)
    inner, outer = lax.rem(rho + RADIALS - 1, RADIALS), lax.rem(rho + 1, RADIALS)
    all_but_one = pl.ds(0, SECTORS - 1)

    def remote(src, dst, send, recv, **where):
        return pltpu.make_async_remote_copy(
            src_ref=src, dst_ref=dst, send_sem=send, recv_sem=recv, device_id=where, device_id_type=pl.DeviceIdType.MESH
        )

    def others(body):
        def step(i, carry):
            body(i)
            return carry

        lax.fori_loop(1, SECTORS, step, 0)

    low, inside, high = pl.ds(0, R), pl.ds(R, (T - 2) * R), pl.ds(T * R - R, R)
    loads = [
        pltpu.make_async_copy(src, dst, load_sem.at[n])
        for n, (src, dst) in enumerate(
            [
                (dens_hbm.at[inside], dext.at[pl.ds(2 * R, (T - 2) * R)]),
                (heat_hbm, heat),
                (swirl_hbm.at[inside], sext.at[pl.ds(2 * R, (T - 2) * R)]),
                (azimuth_hbm, azimuth),
                (radius_hbm, radius),
                (sines_hbm, sines),
                (ac_hbm, acx.at[:, pl.ds(8, T)]),
                (lam_hbm, lam),
                (pick_hbm, pick),
                (base_hbm, base),
                (fwd_hbm, fwd),
                (bwd_hbm, bwd),
                (impedance_hbm, impedance),
                (impedance_hbm, topmost),
                (dens_hbm.at[low], dext.at[pl.ds(R, R)]),
                (dens_hbm.at[high], dext.at[pl.ds(T * R, R)]),
                (swirl_hbm.at[low], sext.at[pl.ds(R, R)]),
                (swirl_hbm.at[high], sext.at[pl.ds(T * R, R)]),
            ]
        )
    ]
    barrier = pltpu.get_barrier_semaphore()

    def greet(i):
        pl.semaphore_signal(barrier, inc=1, device_id={"sector": lax.rem(s + i, SECTORS)}, device_id_type=pl.DeviceIdType.MESH)
        pl.semaphore_signal(barrier, inc=1, device_id={"radial": lax.rem(rho + i, RADIALS)}, device_id_type=pl.DeviceIdType.MESH)

    others(greet)
    for load in loads[14:] + loads[:7]:
        load.start()
    pl.semaphore_wait(barrier, 2 * (SECTORS - 1))

    head, tail = pl.ds(0, R), pl.ds(T * R + R, R)
    azimuth_halos = [
        remote(dext.at[pl.ds(R, R)], dext.at[tail], halo_s.at[0], halo_r.at[0], sector=before),
        remote(dext.at[pl.ds(T * R, R)], dext.at[head], halo_s.at[1], halo_r.at[1], sector=after),
        remote(sext.at[pl.ds(R, R)], sext.at[tail], halo_s.at[2], halo_r.at[2], sector=before),
        remote(sext.at[pl.ds(T * R, R)], sext.at[head], halo_s.at[3], halo_r.at[3], sector=after),
    ]
    wave_halos = [
        remote(ac_hbm.at[:, pl.ds(0, 8)], acx.at[:, pl.ds(T + 8, 8)], halo_s.at[4], halo_r.at[4], sector=before),
        remote(ac_hbm.at[:, pl.ds(T - 8, 8)], acx.at[:, pl.ds(0, 8)], halo_s.at[5], halo_r.at[5], sector=after),
    ]
    to_inner = remote(dr.at[1], dr.at[R + 1], halo_s.at[6], halo_r.at[6], radial=inner)
    to_outer = remote(dr.at[R], dr.at[0], halo_s.at[7], halo_r.at[7], radial=outer)
    for load in loads[14:]:
        load.wait()
    for copy in azimuth_halos:
        copy.start()
    loads[0].wait()
    dr[1] = dext[pl.ds(R, T, stride=R), :]
    dr[R] = dext[pl.ds(2 * R - 1, T, stride=R), :]

    @pl.when(rho > 0)
    def _():
        to_inner.start()

    @pl.when(rho < RADIALS - 1)
    def _():
        to_outer.start()

    for copy in wave_halos:
        copy.start()
    loads[1].wait()

    def heat_row(r, total):
        d = dext[pl.ds(R + r, T, stride=R), :]
        dr[r + 1] = d
        return total + heat[pl.ds(r, T, stride=R), :] * d * d

    ends = heat[pl.ds(0, T, stride=R), :] * dr[1] * dr[1] + heat[pl.ds(R - 1, T, stride=R), :] * dr[R] * dr[R]
    hext[8 : 8 + T, :] = lax.fori_loop(1, R - 1, heat_row, ends, unroll=2) * (1.0 / NR)
    heat_halos = [
        remote(hext.at[pl.ds(8, 8)], hext.at[pl.ds(T + 8, 8)], halo_s.at[8], halo_r.at[8], sector=before),
        remote(hext.at[pl.ds(T, 8)], hext.at[pl.ds(0, 8)], halo_s.at[9], halo_r.at[9], sector=after),
    ]
    for copy in heat_halos:
        copy.start()
    for load in loads[7:14]:
        load.start()

    for n in (3, 4, 5, 2):
        loads[n].wait()
    theta = lax.broadcasted_iota(jnp.int32, (T, NZ), 0)
    first = azimuth[s]
    tmask[...] = jnp.where((theta >= first) & (theta < first + MOUTH), 1.0, 0.0).astype(F32)
    lane = lax.broadcasted_iota(jnp.int32, (T, NZ), 1)
    for copy in azimuth_halos:
        copy.wait_recv()

    sine_pair = (sines[0], sines[1])

    def flow_row(i, carry):
        r = lax.rem(i + R - EDGE, R)
        d = dr[r + 1]
        up = dext[pl.ds(2 * R + r, T, stride=R), :]
        down = dext[pl.ds(r, T, stride=R), :]
        axial = jnp.where(lane < NZ - 1, pltpu.roll(d, NZ - 1, 1), 0.0) + jnp.where(lane > 0, pltpu.roll(d, 1, 1), 0.0)
        laplace = (up + down) + (dr[r] + dr[r + 2]) + axial - 6.0 * d
        flux = sext[pl.ds(2 * R + r, T, stride=R), :] * up - sext[pl.ds(r, T, stride=R), :] * down
        where = rho * R + r - radius[s]
        mouth = jnp.where((where >= 0) & (where < MOUTH), 2.5, 0.0).astype(F32)
        change = 0.05 * laplace - 0.5 * flux + (mouth * tmask[...]) * (1.0 - d)
        dn[pl.ds(r, T, stride=R), :] = d + 0.2 * change
        lines = product(sine_pair, split(change), ((1,), (1,)))
        send1[:, i] = lines.reshape(SECTORS, Q, T)
        return carry

    def flow_chunk(c):
        start, count = SENDS[c]
        lax.fori_loop(start, start + count, flow_row, 0)
        part = pl.ds(start, count)

        def go(i):
            peer = lax.rem(s + i, SECTORS)
            remote(send1.at[peer, part], recv1.at[s, part], f_s.at[c], f_r.at[c], sector=peer).start()

        others(go)
        recv1[s, part] = send1[s, part]

    def forward_all(c):
        part = pl.ds(*SENDS[c])
        return remote(send1.at[all_but_one, part], recv1.at[all_but_one, part], f_s.at[c], f_r.at[c], sector=after)

    def backward_all(c):
        part = pl.ds(*RETURNS[c])
        return remote(send2.at[all_but_one, part], recv2.at[all_but_one, part], b_s.at[c], b_r.at[c], sector=after)

    def tile_rows(peer):
        return pl.ds(pl.multiple_of(8 * peer, 8), 24)

    def share_heat(i):
        peer = lax.rem(rho + i, RADIALS)
        remote(hext.at[tile_rows(peer)], srcbuf.at[rho], few_s.at[0], few_r.at[0], radial=peer).start()

    def share_wave(i):
        peer = lax.rem(rho + i, RADIALS)
        remote(agbuf.at[rho], agbuf.at[rho], few_s.at[1], few_r.at[1], radial=peer).start()

    def share_press(i):
        peer = lax.rem(s + i, SECTORS)
        remote(psend.at[peer], precv.at[s], few_s.at[2], few_r.at[2], sector=peer).start()

    all_heat = remote(srcbuf.at[all_but_one], srcbuf.at[all_but_one], few_s.at[0], few_r.at[0], radial=outer)
    all_wave = remote(agbuf.at[all_but_one], agbuf.at[all_but_one], few_s.at[1], few_r.at[1], radial=outer)
    all_press = remote(psend.at[all_but_one], precv.at[all_but_one], few_s.at[2], few_r.at[2], sector=after)

    flow_chunk(0)

    @pl.when(rho > 0)
    def _():
        to_outer.wait_recv()

    @pl.when(rho == 0)
    def _():
        dr[0] = jnp.zeros((T, NZ), F32)

    @pl.when(rho < RADIALS - 1)
    def _():
        to_inner.wait_recv()

    @pl.when(rho == RADIALS - 1)
    def _():
        dr[R + 1] = jnp.zeros((T, NZ), F32)

    for copy in heat_halos + wave_halos:
        copy.wait_recv()
    others(share_heat)
    srcbuf[rho] = hext[tile_rows(rho), :]

    for c in range(1, EDGE_SENDS):
        flow_chunk(c)

    loads[6].wait()
    all_heat.wait_recv()
    source = srcbuf[0]
    for i in range(1, RADIALS):
        source = source + srcbuf[i]
    source = 0.5 * source
    lane24 = lax.broadcasted_iota(jnp.int32, (24, NZ), 1)
    p, u, w = (acx[n, tile_rows(rho), :] for n in range(3))
    for _ in range(SUBSTEPS):
        u = u - 0.5 * (pltpu.roll(p, 23, 0) - p)
        w = w - 0.5 * (jnp.where(lane24 < NZ - 1, pltpu.roll(p, NZ - 1, 1), 0.0) - p)
        along, axial = u - pltpu.roll(u, 1, 0), w - jnp.where(lane24 > 0, pltpu.roll(w, 1, 1), 0.0)
        p = p - 0.5 * (along + axial) + source
    for n, field in enumerate((p, u, w)):
        agbuf[rho, n] = field[8:16]
    others(share_wave)

    flow_chunk(EDGE_SENDS)

    all_wave.wait_recv()
    for n in range(3):
        acn[n] = agbuf[:, n].reshape(T, NZ)
    psend[...] = product(sine_pair, split(0.5 * acn[0]), ((1,), (1,))).reshape(SECTORS, Q, T)
    others(share_press)
    precv[s] = psend[s]

    flow_chunk(EDGE_SENDS + 1)

    for n in (7, 8, 9, 12, 13):
        loads[n].wait()
    whole = jnp.concatenate([impedance[0 : NT // 2].reshape(Q, T), jnp.full((Q, T), topmost[NT // 2], F32)], 0)
    top = whole.astype(BF16)
    rest = whole - top.astype(F32)
    middle = rest.astype(BF16)
    bottom = (rest - middle.astype(F32)).astype(BF16)

    def diagonal_of(k, carry):
        at = pl.ds(pl.multiple_of(k * WIDE, WIDE), WIDE)
        picked = [
            lax.dot_general(part, pick[0:T, at], (((1,), (0,)), ((), ())), preferred_element_type=F32) for part in (top, middle, bottom)
        ]
        chosen = (picked[0] + picked[1] + picked[2]) * pick[T : T + 2 * Q, at].astype(F32)
        one = 1.0 / (base[0:1, at] + jnp.sum(chosen, axis=0, keepdims=True))
        inverse[0, :, at] = jnp.broadcast_to(one, (Q, WIDE))
        inverse[1, :, at] = jnp.broadcast_to(one * base[1:2, at], (Q, WIDE))
        return carry

    lax.fori_loop(0, TILES, diagonal_of, 0, unroll=2)
    loads[10].wait()

    def keep(row, low, values):
        cosines, odds = values
        for k in range(TILES):
            pair = (cosines[0], cosines[8]) if k == 0 else (cosines[k], odds[k])
            for half, value in enumerate(pair):
                for at, part in zip((row, low), split(value)):
                    y[k, pl.ds(at, 2 * Q), T * half : T * half + T] = part

    def first_stage(x):
        e = [x[0]] + [x[n] + x[SECTORS - n] for n in range(1, 8)] + [x[8]]
        return cosine_stage(e), sine_stage([None] + [x[n] - x[SECTORS - n] for n in range(1, 8)])

    def mode_lanes(k):
        return pl.ds(pl.multiple_of(k * WIDE, WIDE), WIDE)

    def forward_rows(start, count, place, offset, extra):
        total = count + (2 if extra else 0)

        def pair(i, carry):
            x = [recv1[n, pl.ds(start + 2 * i, 2)].reshape(2 * Q, T) for n in range(SECTORS)]
            row = pl.multiple_of(offset + 2 * Q * i, 2 * Q)
            keep(row, pl.multiple_of(row + total * Q, 2 * Q), first_stage(x))
            return carry

        lax.fori_loop(0, count // 2, pair, 0)
        if extra:
            x = [jnp.concatenate([precv[n], precv[n]], 0) for n in range(SECTORS)]
            keep(offset + count * Q, offset + count * Q + total * Q, first_stage(x))

        def tile(k, carry):
            out = stacked(y.at[k], pl.ds(offset, 2 * total * Q), total * Q, pl.ds(0, WIDE), (fwd[0, k], fwd[1, k]))
            for begin, amount, target in place:
                modes[pl.ds(REACH + target, amount), :, mode_lanes(k)] = out[begin * Q : (begin + amount) * Q].reshape(amount, Q, WIDE)
            if extra:
                phat[:, mode_lanes(k)] = out[count * Q : count * Q + Q]
            return carry

        lax.fori_loop(0, TILES, tile, 0, unroll=True)

    modes_inner = remote(modes.at[pl.ds(REACH, REACH)], modes.at[pl.ds(REACH + R, REACH)], halo_s.at[10], halo_r.at[10], radial=inner)
    modes_outer = remote(modes.at[pl.ds(R, REACH)], modes.at[pl.ds(0, REACH)], halo_s.at[11], halo_r.at[11], radial=outer)

    for c in range(EDGE_SENDS):
        forward_all(c).wait_recv()
    forward_rows(0, 2 * EDGE, ((0, EDGE, R - EDGE), (EDGE, EDGE, 0)), 0, False)

    @pl.when(rho > 0)
    def _():
        modes_inner.start()

    @pl.when(rho < RADIALS - 1)
    def _():
        modes_outer.start()

    axial_sum = lam[pl.ds(pl.multiple_of(s * Q, Q), Q), :]
    keep_low = jnp.where(rho > 0, 1.0, 0.0).astype(F32)
    keep_high = jnp.where(rho < RADIALS - 1, 1.0, 0.0).astype(F32)

    def solve_rows(start, stop, groups):
        rows = range(start - REACH, stop + REACH)

        def block(b, carry):
            at = pl.ds(pl.multiple_of(b * T, T), T)
            inv, last, extra = inverse[0, :, at], inverse[1, :, at], phat[:, at]
            low, high = (inv * keep_low, extra * keep_low), (inv * keep_high, extra * keep_high)
            side = {r: low if r < 0 else high if r >= R else (inv, extra) for r in rows}
            c = {r: modes[r + REACH, :, at] + side[r][1] for r in rows}
            x = {r: c[r] * side[r][0] for r in rows}
            for sweep in range(1, SWEEPS):
                x = {
                    r: ((c[r] + axial_sum * x[r]) + (x[r - 1] + x[r + 1])) * (last if sweep == SWEEPS - 1 else side[r][0])
                    for r in range(start - REACH + sweep, stop + REACH - sweep)
                }
            for begin, amount in groups:
                for n in range(0, amount, 2):
                    row = 2 * begin * Q + n * Q
                    for place, part in zip((row, row + amount * Q), split(jnp.concatenate([x[begin + n], x[begin + n + 1]], 0))):
                        x2[place : place + 2 * Q, at] = part
            return carry

        lax.fori_loop(0, NT // T, block, 0)

    def backward_chunk(c):
        start, count = RETURNS[c]

        def tile(k, carry):
            zbuf[k, pl.ds(start * Q, count * Q), :] = stacked(
                x2, pl.ds(2 * start * Q, 2 * count * Q), count * Q, mode_lanes(k), (bwd[0, k], bwd[1, k])
            )
            return carry

        lax.fori_loop(0, TILES, tile, 0, unroll=True)

        def row(r, carry):
            at = pl.ds(pl.multiple_of(r * Q, Q), Q)
            z = [(zbuf[k, at, 0:T], zbuf[k, at, T:WIDE]) for k in range(TILES)]
            even = cosine_stage([z[0][0]] + [z[k][0] for k in range(1, TILES)] + [z[0][1]])
            odd = sine_stage([None] + [z[k][1] for k in range(1, TILES)])
            send2[0, r], send2[8, r] = even[0], even[8]
            for n in range(1, 8):
                send2[n, r] = even[n] + odd[n]
                send2[SECTORS - n, r] = even[n] - odd[n]
            return carry

        lax.fori_loop(start, start + count, row, 0, unroll=2)
        part = pl.ds(start, count)

        def go(i):
            peer = lax.rem(s + i, SECTORS)
            remote(send2.at[peer, part], recv2.at[s, part], b_s.at[c], b_r.at[c], sector=peer).start()

        others(go)
        recv2[s, part] = send2[s, part]

    forward_all(EDGE_SENDS).wait_recv()
    all_press.wait_recv()
    forward_rows(2 * EDGE, MIDDLE, ((0, MIDDLE, EDGE),), Y_MIDDLE, True)

    @pl.when(rho > 0)
    def _():
        modes_outer.wait_recv()

    @pl.when(rho == 0)
    def _():
        modes[0:REACH] = jnp.zeros((REACH, Q, NT), F32)

    solve_rows(0, RETURNS[0][1], RETURNS[:1])
    loads[11].wait()
    backward_chunk(0)

    forward_all(EDGE_SENDS + 1).wait_recv()
    forward_rows(2 * EDGE + MIDDLE, REST, ((0, REST, EDGE + MIDDLE),), Y_MIDDLE + 2 * (MIDDLE + 2) * Q, False)

    @pl.when(rho < RADIALS - 1)
    def _():
        modes_inner.wait_recv()

    @pl.when(rho == RADIALS - 1)
    def _():
        modes[REACH + R : R + 2 * REACH] = jnp.zeros((REACH, Q, NT), F32)

    for c in range(1, len(RETURNS)):
        start, count = RETURNS[c]
        solve_rows(start, start + count, RETURNS[c : c + 1])
        backward_chunk(c)

    for copy in azimuth_halos + wave_halos + heat_halos + [all_heat, all_wave, all_press] + [forward_all(c) for c in range(len(SENDS))]:
        copy.wait_send()

    @pl.when(rho > 0)
    def _():
        to_inner.wait_send()
        modes_inner.wait_send()

    @pl.when(rho < RADIALS - 1)
    def _():
        to_outer.wait_send()
        modes_outer.wait_send()

    def finish(r, carry):
        lines = recv2[:, r].reshape(NZ, T).T
        press[pl.ds(r, T, stride=R), :] = product(split(lines), sine_pair)
        return carry

    for c, (start, count) in enumerate(RETURNS):
        backward_all(c).wait_recv()
        lax.fori_loop(start, start + count, finish, 0, unroll=2)
    for c in range(len(RETURNS)):
        backward_all(c).wait_send()


def deliver(dn, press, acn, dn_hbm, press_hbm, acn_hbm, sem):
    copies = [pltpu.make_async_copy(*pair, sem.at[n]) for n, pair in enumerate(((dn, dn_hbm), (press, press_hbm), (acn, acn_hbm)))]
    for copy in copies:
        copy.start()
    for copy in copies:
        copy.wait()


def shards(density, swirl, heat_rate, acoustic, mode_impedance, mouth_azimuth, mouth_radius):
    tiles, mode, weight = mode_tables()
    sines, axial_sum = axial_tables()
    pick = np.concatenate([np.arange(T)[:, None] == mode[None, :] % T, np.arange(2 * Q)[:, None] == mode[None, :] // T]).astype(BF16)
    base = np.stack([4.0 + 2.0 - 2.0 * np.cos(2 * np.pi * mode / NT), weight]).astype(np.float32)
    base = np.concatenate([base, np.zeros((6, NT), np.float32)])
    lam = np.repeat(axial_sum[:, None], T, 1).astype(np.float32)
    flat = lambda x: x.reshape(T * R, NZ)
    pinned = lambda x: pltpu.with_memory_space_constraint(jnp.asarray(x), pltpu.HBM)
    vmem, anywhere = pl.BlockSpec(memory_space=pltpu.VMEM), pl.BlockSpec(memory_space=pltpu.HBM)
    dma = pltpu.SemaphoreType.DMA
    fields = [density, swirl, heat_rate]
    dn, press, acn = pl.pallas_call(
        kernel,
        out_shape=(
            jax.ShapeDtypeStruct((T * R, NZ), F32),
            jax.ShapeDtypeStruct((T * R, NZ), F32),
            jax.ShapeDtypeStruct((3, T, NZ), F32),
        ),
        in_specs=[anywhere] * 13,
        out_specs=(vmem, vmem, vmem),
        scratch_shapes=[
            pltpu.SMEM((BURNERS,), jnp.int32),
            pltpu.SMEM((BURNERS,), jnp.int32),
            pltpu.VMEM((NT // 2 + 1,), F32),
            pltpu.SMEM((NT // 2 + 1,), F32),
            pltpu.VMEM(((T + 2) * R, NZ), F32),
            pltpu.VMEM(((T + 2) * R, NZ), F32),
            pltpu.VMEM((T * R, NZ), F32),
            pltpu.VMEM((R + 2, T, NZ), F32),
            pltpu.VMEM((3, T + 16, NZ), F32),
            pltpu.VMEM((T + 16, NZ), F32),
            pltpu.VMEM((T, NZ), F32),
            pltpu.VMEM((RADIALS, 24, NZ), F32),
            pltpu.VMEM((RADIALS, 3, 8, NZ), F32),
            pltpu.VMEM((SECTORS, Q, T), F32),
            pltpu.VMEM((SECTORS, Q, T), F32),
            pltpu.VMEM((Q, NT), F32),
            pltpu.VMEM((SECTORS, R, Q, T), F32),
            pltpu.VMEM((SECTORS, R, Q, T), F32),
            pltpu.VMEM((SECTORS, R, Q, T), F32),
            pltpu.VMEM((SECTORS, R, Q, T), F32),
            pltpu.VMEM((R + 2 * REACH, Q, NT), F32),
            pltpu.VMEM((TILES, 2 * (R + 2) * Q, WIDE), BF16),
            pltpu.VMEM((2 * R * Q, NT), BF16),
            pltpu.VMEM((TILES, R * Q, WIDE), F32),
            pltpu.VMEM((2, Q, NT), F32),
            pltpu.VMEM((NZ, T), F32),
            pltpu.VMEM((2, NZ, NZ), BF16),
            pltpu.VMEM((T + 2 * Q, NT), BF16),
            pltpu.VMEM((8, NT), F32),
            pltpu.VMEM((2, TILES, WIDE, WIDE), BF16),
            pltpu.VMEM((2, TILES, WIDE, WIDE), BF16),
            dma((18,)),
            dma((12,)),
            dma((12,)),
            dma((3,)),
            dma((3,)),
            dma((len(SENDS),)),
            dma((len(SENDS),)),
            dma((len(RETURNS),)),
            dma((len(RETURNS),)),
        ],
        compiler_params=pltpu.CompilerParams(collective_id=0, has_side_effects=True, vmem_limit_bytes=VMEM_LIMIT),
    )(
        pinned(mouth_azimuth), pinned(mouth_radius), pinned(mode_impedance), *[pinned(flat(x)) for x in fields], pinned(acoustic), pinned(lam),
        pinned(halves(sines)), pinned(pick), pinned(base), pinned(halves(tiles)), pinned(halves(tiles.transpose(0, 2, 1))),
    )
    results = (dn, press, acn)
    dn, press, acn = pl.pallas_call(
        deliver,
        out_shape=tuple(jax.ShapeDtypeStruct(x.shape, F32) for x in results),
        in_specs=[vmem] * 3,
        out_specs=(anywhere,) * 3,
        scratch_shapes=[dma((3,))],
        compiler_params=pltpu.CompilerParams(vmem_limit_bytes=2**20),
    )(*results)
    return dn.reshape(T, R, NZ), press.reshape(T, R, NZ), acn


def solution(mesh):
    cells, columns = P("sector", "radial", None), P(None, "sector", None)
    return jax.shard_map(
        shards,
        mesh=mesh,
        in_specs=(cells, cells, cells, columns, P(), P(), P()),
        out_specs=(cells, cells, columns),
        check_vma=False,
    )
```

```python
import math

import jax
import jax.numpy as jnp
import numpy as np
from jax import lax
from jax.experimental import pallas as pl
from jax.experimental.pallas import tpu as pltpu
from jax.sharding import PartitionSpec as P

MOUTH = 8
SWEEPS = 4
SUBSTEPS = 8
REACH = SWEEPS - 1
NT, NR, NZ = 2048, 256, 128
SECTORS, RADIALS = 16, 16
T = NT // SECTORS
R = NR // RADIALS
Q = NZ // SECTORS
TILES = 8
WIDE = 2 * T
BURNERS = 16
EDGE = 4
SENDS = ((0, 1), (1, 3), (4, 4), (8, 4), (12, 4))
RETURNS = ((0, 4), (4, 4), (8, 6), (14, 2))
Y_MIDDLE = 4 * EDGE * Q
EDGE_SENDS, MIDDLE = 3, 4
REST = R - 2 * EDGE - MIDDLE
VMEM_LIMIT = 48 * 2**20

F32, BF16 = jnp.float32, jnp.bfloat16


def halves(table):
    high = table.astype(BF16)
    low = (table - high.astype(np.float64)).astype(BF16)
    return np.stack([high, low])


def mode_tables():
    j = np.arange(T)
    a = np.arange(T)
    tiles = np.zeros((TILES, WIDE, WIDE))
    mode = np.zeros((TILES, WIDE), np.int64)
    for k in range(1, TILES):
        order = SECTORS * a + k
        phase = 2 * np.pi * ((j[:, None] * order[None, :]) % NT) / NT
        tiles[k, :T, :T], tiles[k, :T, T:] = np.cos(phase), np.sin(phase)
        tiles[k, T:, :T], tiles[k, T:, T:] = -np.sin(phase), np.cos(phase)
        mode[k] = np.concatenate([order, order])
    low_cos, low_sin = SECTORS * np.arange(T // 2 + 1), SECTORS * np.arange(1, T // 2)
    mid = SECTORS * np.arange(T // 2) + SECTORS // 2

    def phase_of(order):
        return 2 * np.pi * ((j[:, None] * order[None, :]) % NT) / NT

    tiles[0, :T, :T] = np.concatenate([np.cos(phase_of(low_cos)), np.sin(phase_of(low_sin))], 1)
    tiles[0, T:, T:] = np.concatenate([np.cos(phase_of(mid)), np.sin(phase_of(mid))], 1)
    mode[0] = np.concatenate([low_cos, low_sin, mid, mid])
    mode = np.minimum(mode, NT - mode)
    weight = np.where((mode == 0) | (mode == NT // 2), 1.0, 2.0) / NT
    return tiles, mode.reshape(-1), weight.reshape(-1)


def axial_tables():
    n = np.arange(1, NZ + 1)
    sines = math.sqrt(2.0 / (NZ + 1)) * np.sin(np.pi * ((n[:, None] * n[None, :]) % (2 * (NZ + 1))) / (NZ + 1))
    return sines, 2.0 * np.cos(np.pi * n / (NZ + 1))


C1, C2, C3 = (math.cos(math.pi * n / 8) for n in (1, 2, 3))


def cosine_stage(e):
    f = [e[n] + e[8 - n] for n in range(4)] + [e[4]]
    g = [e[n] - e[8 - n] for n in range(4)]
    outer, inner = f[0] + f[4], f[1] + f[3]
    differ, h = f[0] - f[4], C2 * (f[1] - f[3])
    both = outer + f[2]
    w = C2 * g[2]
    up, down = g[0] + w, g[0] - w
    b, c = C1 * g[1] + C3 * g[3], C3 * g[1] - C1 * g[3]
    return [both + inner, up + b, differ + h, down + c, outer - f[2], down - c, differ - h, up - b, both - inner]


def sine_stage(o):
    u = [None] + [o[n] + o[8 - n] for n in (1, 2, 3)] + [o[4]]
    v = [None] + [o[n] - o[8 - n] for n in (1, 2, 3)]
    h = C2 * (v[1] + v[3])
    w = C2 * u[2]
    up, down = w + u[4], w - u[4]
    b, c = C3 * u[1] + C1 * u[3], C1 * u[1] - C3 * u[3]
    return [None, b + up, h + v[2], c + down, v[1] - v[3], c - down, h - v[2], b - up]


def split(x):
    high = x.astype(BF16)
    return high, (x - high.astype(F32)).astype(BF16)


def product(left, right, dims=((1,), (0,))):
    def one(a, b):
        return lax.dot_general(a, b, (dims, ((), ())), preferred_element_type=F32)

    return one(left[0], right[0]) + (one(left[0], right[1]) + one(left[1], right[0]))


def stacked(ref, rows, half, lanes, right):
    both = lax.dot_general(ref[rows, lanes], right[0], (((1,), (0,)), ((), ())), preferred_element_type=F32)
    high = ref[pl.ds(rows.start, half), lanes]
    return both[:half] + (both[half:] + lax.dot_general(high, right[1], (((1,), (0,)), ((), ())), preferred_element_type=F32))


def kernel(
    azimuth_hbm, radius_hbm, impedance_hbm, dens_hbm, swirl_hbm, heat_hbm, ac_hbm, lam_hbm, sines_hbm, pick_hbm, base_hbm, fwd_hbm, bwd_hbm,
    dn, press, acn,
    azimuth, radius, impedance, topmost, dext, sext, heat, dr, acx, hext, tmask, srcbuf, agbuf, psend, precv, phat,
    send1, recv1, send2, recv2, modes, y, x2, zbuf, inverse, lam, sines, pick, base, fwd, bwd,
    load_sem, halo_s, halo_r, few_s, few_r, f_s, f_r, b_s, b_r,
):
    s, rho = lax.axis_index("sector"), lax.axis_index("radial")
    after, before = lax.rem(s + 1, SECTORS), lax.rem(s + SECTORS - 1, SECTORS)
    inner, outer = lax.rem(rho + RADIALS - 1, RADIALS), lax.rem(rho + 1, RADIALS)
    all_but_one = pl.ds(0, SECTORS - 1)

    def remote(src, dst, send, recv, **where):
        return pltpu.make_async_remote_copy(
            src_ref=src, dst_ref=dst, send_sem=send, recv_sem=recv, device_id=where, device_id_type=pl.DeviceIdType.MESH
        )

    def others(body):
        def step(i, carry):
            body(i)
            return carry

        lax.fori_loop(1, SECTORS, step, 0)

    low, inside, high = pl.ds(0, R), pl.ds(R, (T - 2) * R), pl.ds(T * R - R, R)
    loads = [
        pltpu.make_async_copy(src, dst, load_sem.at[n])
        for n, (src, dst) in enumerate(
            [
                (dens_hbm.at[inside], dext.at[pl.ds(2 * R, (T - 2) * R)]),
                (heat_hbm, heat),
                (swirl_hbm.at[inside], sext.at[pl.ds(2 * R, (T - 2) * R)]),
                (azimuth_hbm, azimuth),
                (radius_hbm, radius),
                (sines_hbm, sines),
                (ac_hbm, acx.at[:, pl.ds(8, T)]),
                (lam_hbm, lam),
                (pick_hbm, pick),
                (base_hbm, base),
                (fwd_hbm, fwd),
                (bwd_hbm, bwd),
                (impedance_hbm, impedance),
                (impedance_hbm, topmost),
                (dens_hbm.at[low], dext.at[pl.ds(R, R)]),
                (dens_hbm.at[high], dext.at[pl.ds(T * R, R)]),
                (swirl_hbm.at[low], sext.at[pl.ds(R, R)]),
                (swirl_hbm.at[high], sext.at[pl.ds(T * R, R)]),
            ]
        )
    ]
    barrier = pltpu.get_barrier_semaphore()

    def greet(i):
        pl.semaphore_signal(barrier, inc=1, device_id={"sector": lax.rem(s + i, SECTORS)}, device_id_type=pl.DeviceIdType.MESH)
        pl.semaphore_signal(barrier, inc=1, device_id={"radial": lax.rem(rho + i, RADIALS)}, device_id_type=pl.DeviceIdType.MESH)

    others(greet)
    for load in loads[14:] + loads[:7]:
        load.start()
    pl.semaphore_wait(barrier, 2 * (SECTORS - 1))

    head, tail = pl.ds(0, R), pl.ds(T * R + R, R)
    azimuth_halos = [
        remote(dext.at[pl.ds(R, R)], dext.at[tail], halo_s.at[0], halo_r.at[0], sector=before),
        remote(dext.at[pl.ds(T * R, R)], dext.at[head], halo_s.at[1], halo_r.at[1], sector=after),
        remote(sext.at[pl.ds(R, R)], sext.at[tail], halo_s.at[2], halo_r.at[2], sector=before),
        remote(sext.at[pl.ds(T * R, R)], sext.at[head], halo_s.at[3], halo_r.at[3], sector=after),
    ]
    wave_halos = [
        remote(ac_hbm.at[:, pl.ds(0, 8)], acx.at[:, pl.ds(T + 8, 8)], halo_s.at[4], halo_r.at[4], sector=before),
        remote(ac_hbm.at[:, pl.ds(T - 8, 8)], acx.at[:, pl.ds(0, 8)], halo_s.at[5], halo_r.at[5], sector=after),
    ]
    to_inner = remote(dr.at[1], dr.at[R + 1], halo_s.at[6], halo_r.at[6], radial=inner)
    to_outer = remote(dr.at[R], dr.at[0], halo_s.at[7], halo_r.at[7], radial=outer)
    for load in loads[14:]:
        load.wait()
    for copy in azimuth_halos:
        copy.start()
    loads[0].wait()
    dr[1] = dext[pl.ds(R, T, stride=R), :]
    dr[R] = dext[pl.ds(2 * R - 1, T, stride=R), :]

    @pl.when(rho > 0)
    def _():
        to_inner.start()

    @pl.when(rho < RADIALS - 1)
    def _():
        to_outer.start()

    for copy in wave_halos:
        copy.start()
    loads[1].wait()

    def heat_row(r, total):
        d = dext[pl.ds(R + r, T, stride=R), :]
        dr[r + 1] = d
        return total + heat[pl.ds(r, T, stride=R), :] * d * d

    ends = heat[pl.ds(0, T, stride=R), :] * dr[1] * dr[1] + heat[pl.ds(R - 1, T, stride=R), :] * dr[R] * dr[R]
    hext[8 : 8 + T, :] = lax.fori_loop(1, R - 1, heat_row, ends, unroll=2) * (1.0 / NR)
    heat_halos = [
        remote(hext.at[pl.ds(8, 8)], hext.at[pl.ds(T + 8, 8)], halo_s.at[8], halo_r.at[8], sector=before),
        remote(hext.at[pl.ds(T, 8)], hext.at[pl.ds(0, 8)], halo_s.at[9], halo_r.at[9], sector=after),
    ]
    for copy in heat_halos:
        copy.start()
    for load in loads[7:14]:
        load.start()

    for n in (3, 4, 5, 2):
        loads[n].wait()
    theta = lax.broadcasted_iota(jnp.int32, (T, NZ), 0)
    first = azimuth[s]
    tmask[...] = jnp.where((theta >= first) & (theta < first + MOUTH), 1.0, 0.0).astype(F32)
    lane = lax.broadcasted_iota(jnp.int32, (T, NZ), 1)
    for copy in azimuth_halos:
        copy.wait_recv()

    sine_pair = (sines[0], sines[1])

    def flow_row(i, carry):
        r = lax.rem(i + R - EDGE, R)
        d = dr[r + 1]
        up = dext[pl.ds(2 * R + r, T, stride=R), :]
        down = dext[pl.ds(r, T, stride=R), :]
        axial = jnp.where(lane < NZ - 1, pltpu.roll(d, NZ - 1, 1), 0.0) + jnp.where(lane > 0, pltpu.roll(d, 1, 1), 0.0)
        laplace = (up + down) + (dr[r] + dr[r + 2]) + axial - 6.0 * d
        flux = sext[pl.ds(2 * R + r, T, stride=R), :] * up - sext[pl.ds(r, T, stride=R), :] * down
        where = rho * R + r - radius[s]
        mouth = jnp.where((where >= 0) & (where < MOUTH), 2.5, 0.0).astype(F32)
        change = 0.05 * laplace - 0.5 * flux + (mouth * tmask[...]) * (1.0 - d)
        dn[pl.ds(r, T, stride=R), :] = d + 0.2 * change
        lines = product(sine_pair, split(change), ((1,), (1,)))
        send1[:, i] = lines.reshape(SECTORS, Q, T)
        return carry

    def flow_chunk(c):
        start, count = SENDS[c]
        lax.fori_loop(start, start + count, flow_row, 0)
        part = pl.ds(start, count)

        def go(i):
            peer = lax.rem(s + i, SECTORS)
            remote(send1.at[peer, part], recv1.at[s, part], f_s.at[c], f_r.at[c], sector=peer).start()

        others(go)
        recv1[s, part] = send1[s, part]

    def forward_all(c):
        part = pl.ds(*SENDS[c])
        return remote(send1.at[all_but_one, part], recv1.at[all_but_one, part], f_s.at[c], f_r.at[c], sector=after)

    def backward_all(c):
        part = pl.ds(*RETURNS[c])
        return remote(send2.at[all_but_one, part], recv2.at[all_but_one, part], b_s.at[c], b_r.at[c], sector=after)

    def tile_rows(peer):
        return pl.ds(pl.multiple_of(8 * peer, 8), 24)

    def share_heat(i):
        peer = lax.rem(rho + i, RADIALS)
        remote(hext.at[tile_rows(peer)], srcbuf.at[rho], few_s.at[0], few_r.at[0], radial=peer).start()

    def share_wave(i):
        peer = lax.rem(rho + i, RADIALS)
        remote(agbuf.at[rho], agbuf.at[rho], few_s.at[1], few_r.at[1], radial=peer).start()

    def share_press(i):
        peer = lax.rem(s + i, SECTORS)
        remote(psend.at[peer], precv.at[s], few_s.at[2], few_r.at[2], sector=peer).start()

    all_heat = remote(srcbuf.at[all_but_one], srcbuf.at[all_but_one], few_s.at[0], few_r.at[0], radial=outer)
    all_wave = remote(agbuf.at[all_but_one], agbuf.at[all_but_one], few_s.at[1], few_r.at[1], radial=outer)
    all_press = remote(psend.at[all_but_one], precv.at[all_but_one], few_s.at[2], few_r.at[2], sector=after)

    flow_chunk(0)

    @pl.when(rho > 0)
    def _():
        to_outer.wait_recv()

    @pl.when(rho == 0)
    def _():
        dr[0] = jnp.zeros((T, NZ), F32)

    @pl.when(rho < RADIALS - 1)
    def _():
        to_inner.wait_recv()

    @pl.when(rho == RADIALS - 1)
    def _():
        dr[R + 1] = jnp.zeros((T, NZ), F32)

    for copy in heat_halos + wave_halos:
        copy.wait_recv()
    others(share_heat)
    srcbuf[rho] = hext[tile_rows(rho), :]

    for c in range(1, EDGE_SENDS):
        flow_chunk(c)

    loads[6].wait()
    all_heat.wait_recv()
    source = srcbuf[0]
    for i in range(1, RADIALS):
        source = source + srcbuf[i]
    source = 0.5 * source
    lane24 = lax.broadcasted_iota(jnp.int32, (24, NZ), 1)
    p, u, w = (acx[n, tile_rows(rho), :] for n in range(3))
    for _ in range(SUBSTEPS):
        u = u - 0.5 * (pltpu.roll(p, 23, 0) - p)
        w = w - 0.5 * (jnp.where(lane24 < NZ - 1, pltpu.roll(p, NZ - 1, 1), 0.0) - p)
        along, axial = u - pltpu.roll(u, 1, 0), w - jnp.where(lane24 > 0, pltpu.roll(w, 1, 1), 0.0)
        p = p - 0.5 * (along + axial) + source
    for n, field in enumerate((p, u, w)):
        agbuf[rho, n] = field[8:16]
    others(share_wave)

    flow_chunk(EDGE_SENDS)

    all_wave.wait_recv()
    for n in range(3):
        acn[n] = agbuf[:, n].reshape(T, NZ)
    psend[...] = product(sine_pair, split(0.5 * acn[0]), ((1,), (1,))).reshape(SECTORS, Q, T)
    others(share_press)
    precv[s] = psend[s]

    flow_chunk(EDGE_SENDS + 1)

    for n in (7, 8, 9, 12, 13):
        loads[n].wait()
    whole = jnp.concatenate([impedance[0 : NT // 2].reshape(Q, T), jnp.full((Q, T), topmost[NT // 2], F32)], 0)
    top = whole.astype(BF16)
    rest = whole - top.astype(F32)
    middle = rest.astype(BF16)
    bottom = (rest - middle.astype(F32)).astype(BF16)

    def diagonal_of(k, carry):
        at = pl.ds(pl.multiple_of(k * WIDE, WIDE), WIDE)
        picked = [
            lax.dot_general(part, pick[0:T, at], (((1,), (0,)), ((), ())), preferred_element_type=F32) for part in (top, middle, bottom)
        ]
        chosen = (picked[0] + picked[1] + picked[2]) * pick[T : T + 2 * Q, at].astype(F32)
        one = 1.0 / (base[0:1, at] + jnp.sum(chosen, axis=0, keepdims=True))
        inverse[0, :, at] = jnp.broadcast_to(one, (Q, WIDE))
        inverse[1, :, at] = jnp.broadcast_to(one * base[1:2, at], (Q, WIDE))
        return carry

    lax.fori_loop(0, TILES, diagonal_of, 0, unroll=2)
    loads[10].wait()

    def keep(row, low, values):
        cosines, odds = values
        for k in range(TILES):
            pair = (cosines[0], cosines[8]) if k == 0 else (cosines[k], odds[k])
            for half, value in enumerate(pair):
                for at, part in zip((row, low), split(value)):
                    y[k, pl.ds(at, 2 * Q), T * half : T * half + T] = part

    def first_stage(x):
        e = [x[0]] + [x[n] + x[SECTORS - n] for n in range(1, 8)] + [x[8]]
        return cosine_stage(e), sine_stage([None] + [x[n] - x[SECTORS - n] for n in range(1, 8)])

    def mode_lanes(k):
        return pl.ds(pl.multiple_of(k * WIDE, WIDE), WIDE)

    def forward_rows(start, count, place, offset, extra):
        total = count + (2 if extra else 0)

        def pair(i, carry):
            x = [recv1[n, pl.ds(start + 2 * i, 2)].reshape(2 * Q, T) for n in range(SECTORS)]
            row = pl.multiple_of(offset + 2 * Q * i, 2 * Q)
            keep(row, pl.multiple_of(row + total * Q, 2 * Q), first_stage(x))
            return carry

        lax.fori_loop(0, count // 2, pair, 0, unroll=2)
        if extra:
            x = [jnp.concatenate([precv[n], precv[n]], 0) for n in range(SECTORS)]
            keep(offset + count * Q, offset + count * Q + total * Q, first_stage(x))

        def tile(k, carry):
            out = stacked(y.at[k], pl.ds(offset, 2 * total * Q), total * Q, pl.ds(0, WIDE), (fwd[0, k], fwd[1, k]))
            for begin, amount, target in place:
                modes[pl.ds(REACH + target, amount), :, mode_lanes(k)] = out[begin * Q : (begin + amount) * Q].reshape(amount, Q, WIDE)
            if extra:
                phat[:, mode_lanes(k)] = out[count * Q : count * Q + Q]
            return carry

        lax.fori_loop(0, TILES, tile, 0, unroll=True)

    modes_inner = remote(modes.at[pl.ds(REACH, REACH)], modes.at[pl.ds(REACH + R, REACH)], halo_s.at[10], halo_r.at[10], radial=inner)
    modes_outer = remote(modes.at[pl.ds(R, REACH)], modes.at[pl.ds(0, REACH)], halo_s.at[11], halo_r.at[11], radial=outer)

    for c in range(EDGE_SENDS):
        forward_all(c).wait_recv()
    forward_rows(0, 2 * EDGE, ((0, EDGE, R - EDGE), (EDGE, EDGE, 0)), 0, False)

    @pl.when(rho > 0)
    def _():
        modes_inner.start()

    @pl.when(rho < RADIALS - 1)
    def _():
        modes_outer.start()

    axial_sum = lam[pl.ds(pl.multiple_of(s * Q, Q), Q), :]
    keep_low = jnp.where(rho > 0, 1.0, 0.0).astype(F32)
    keep_high = jnp.where(rho < RADIALS - 1, 1.0, 0.0).astype(F32)

    def solve_rows(start, stop, groups):
        rows = range(start - REACH, stop + REACH)

        def block(b, carry):
            at = pl.ds(pl.multiple_of(b * T, T), T)
            inv, last, extra = inverse[0, :, at], inverse[1, :, at], phat[:, at]
            low, high = (inv * keep_low, extra * keep_low), (inv * keep_high, extra * keep_high)
            side = {r: low if r < 0 else high if r >= R else (inv, extra) for r in rows}
            c = {r: modes[r + REACH, :, at] + side[r][1] for r in rows}
            x = {r: c[r] * side[r][0] for r in rows}
            for sweep in range(1, SWEEPS):
                x = {
                    r: ((c[r] + axial_sum * x[r]) + (x[r - 1] + x[r + 1])) * (last if sweep == SWEEPS - 1 else side[r][0])
                    for r in range(start - REACH + sweep, stop + REACH - sweep)
                }
            for begin, amount in groups:
                for n in range(0, amount, 2):
                    row = 2 * begin * Q + n * Q
                    for place, part in zip((row, row + amount * Q), split(jnp.concatenate([x[begin + n], x[begin + n + 1]], 0))):
                        x2[place : place + 2 * Q, at] = part
            return carry

        lax.fori_loop(0, NT // T, block, 0, unroll=2)

    def backward_chunk(c):
        start, count = RETURNS[c]

        def tile(k, carry):
            zbuf[k, pl.ds(start * Q, count * Q), :] = stacked(
                x2, pl.ds(2 * start * Q, 2 * count * Q), count * Q, mode_lanes(k), (bwd[0, k], bwd[1, k])
            )
            return carry

        lax.fori_loop(0, TILES, tile, 0, unroll=True)

        def row(r, carry):
            at = pl.ds(pl.multiple_of(r * Q, Q), Q)
            z = [(zbuf[k, at, 0:T], zbuf[k, at, T:WIDE]) for k in range(TILES)]
            even = cosine_stage([z[0][0]] + [z[k][0] for k in range(1, TILES)] + [z[0][1]])
            odd = sine_stage([None] + [z[k][1] for k in range(1, TILES)])
            send2[0, r], send2[8, r] = even[0], even[8]
            for n in range(1, 8):
                send2[n, r] = even[n] + odd[n]
                send2[SECTORS - n, r] = even[n] - odd[n]
            return carry

        lax.fori_loop(start, start + count, row, 0, unroll=2)
        part = pl.ds(start, count)

        def go(i):
            peer = lax.rem(s + i, SECTORS)
            remote(send2.at[peer, part], recv2.at[s, part], b_s.at[c], b_r.at[c], sector=peer).start()

        others(go)
        recv2[s, part] = send2[s, part]

    forward_all(EDGE_SENDS).wait_recv()
    all_press.wait_recv()
    forward_rows(2 * EDGE, MIDDLE, ((0, MIDDLE, EDGE),), Y_MIDDLE, True)

    @pl.when(rho > 0)
    def _():
        modes_outer.wait_recv()

    @pl.when(rho == 0)
    def _():
        modes[0:REACH] = jnp.zeros((REACH, Q, NT), F32)

    solve_rows(0, RETURNS[0][1], RETURNS[:1])
    loads[11].wait()
    backward_chunk(0)

    forward_all(EDGE_SENDS + 1).wait_recv()
    forward_rows(2 * EDGE + MIDDLE, REST, ((0, REST, EDGE + MIDDLE),), Y_MIDDLE + 2 * (MIDDLE + 2) * Q, False)

    @pl.when(rho < RADIALS - 1)
    def _():
        modes_inner.wait_recv()

    @pl.when(rho == RADIALS - 1)
    def _():
        modes[REACH + R : R + 2 * REACH] = jnp.zeros((REACH, Q, NT), F32)

    for c in range(1, len(RETURNS)):
        start, count = RETURNS[c]
        solve_rows(start, start + count, RETURNS[c : c + 1])
        backward_chunk(c)

    for copy in azimuth_halos + wave_halos + heat_halos + [all_heat, all_wave, all_press] + [forward_all(c) for c in range(len(SENDS))]:
        copy.wait_send()

    @pl.when(rho > 0)
    def _():
        to_inner.wait_send()
        modes_inner.wait_send()

    @pl.when(rho < RADIALS - 1)
    def _():
        to_outer.wait_send()
        modes_outer.wait_send()

    def finish(r, carry):
        lines = recv2[:, r].reshape(NZ, T).T
        press[pl.ds(r, T, stride=R), :] = product(split(lines), sine_pair)
        return carry

    for c, (start, count) in enumerate(RETURNS):
        backward_all(c).wait_recv()
        lax.fori_loop(start, start + count, finish, 0, unroll=2)
    for c in range(len(RETURNS)):
        backward_all(c).wait_send()


def deliver(dn, press, acn, dn_hbm, press_hbm, acn_hbm, sem):
    copies = [pltpu.make_async_copy(*pair, sem.at[n]) for n, pair in enumerate(((dn, dn_hbm), (press, press_hbm), (acn, acn_hbm)))]
    for copy in copies:
        copy.start()
    for copy in copies:
        copy.wait()


def shards(density, swirl, heat_rate, acoustic, mode_impedance, mouth_azimuth, mouth_radius):
    tiles, mode, weight = mode_tables()
    sines, axial_sum = axial_tables()
    pick = np.concatenate([np.arange(T)[:, None] == mode[None, :] % T, np.arange(2 * Q)[:, None] == mode[None, :] // T]).astype(BF16)
    base = np.stack([4.0 + 2.0 - 2.0 * np.cos(2 * np.pi * mode / NT), weight]).astype(np.float32)
    base = np.concatenate([base, np.zeros((6, NT), np.float32)])
    lam = np.repeat(axial_sum[:, None], T, 1).astype(np.float32)
    flat = lambda x: x.reshape(T * R, NZ)
    pinned = lambda x: pltpu.with_memory_space_constraint(jnp.asarray(x), pltpu.HBM)
    vmem, anywhere = pl.BlockSpec(memory_space=pltpu.VMEM), pl.BlockSpec(memory_space=pltpu.HBM)
    dma = pltpu.SemaphoreType.DMA
    fields = [density, swirl, heat_rate]
    dn, press, acn = pl.pallas_call(
        kernel,
        out_shape=(
            jax.ShapeDtypeStruct((T * R, NZ), F32),
            jax.ShapeDtypeStruct((T * R, NZ), F32),
            jax.ShapeDtypeStruct((3, T, NZ), F32),
        ),
        in_specs=[anywhere] * 13,
        out_specs=(vmem, vmem, vmem),
        scratch_shapes=[
            pltpu.SMEM((BURNERS,), jnp.int32),
            pltpu.SMEM((BURNERS,), jnp.int32),
            pltpu.VMEM((NT // 2 + 1,), F32),
            pltpu.SMEM((NT // 2 + 1,), F32),
            pltpu.VMEM(((T + 2) * R, NZ), F32),
            pltpu.VMEM(((T + 2) * R, NZ), F32),
            pltpu.VMEM((T * R, NZ), F32),
            pltpu.VMEM((R + 2, T, NZ), F32),
            pltpu.VMEM((3, T + 16, NZ), F32),
            pltpu.VMEM((T + 16, NZ), F32),
            pltpu.VMEM((T, NZ), F32),
            pltpu.VMEM((RADIALS, 24, NZ), F32),
            pltpu.VMEM((RADIALS, 3, 8, NZ), F32),
            pltpu.VMEM((SECTORS, Q, T), F32),
            pltpu.VMEM((SECTORS, Q, T), F32),
            pltpu.VMEM((Q, NT), F32),
            pltpu.VMEM((SECTORS, R, Q, T), F32),
            pltpu.VMEM((SECTORS, R, Q, T), F32),
            pltpu.VMEM((SECTORS, R, Q, T), F32),
            pltpu.VMEM((SECTORS, R, Q, T), F32),
            pltpu.VMEM((R + 2 * REACH, Q, NT), F32),
            pltpu.VMEM((TILES, 2 * (R + 2) * Q, WIDE), BF16),
            pltpu.VMEM((2 * R * Q, NT), BF16),
            pltpu.VMEM((TILES, R * Q, WIDE), F32),
            pltpu.VMEM((2, Q, NT), F32),
            pltpu.VMEM((NZ, T), F32),
            pltpu.VMEM((2, NZ, NZ), BF16),
            pltpu.VMEM((T + 2 * Q, NT), BF16),
            pltpu.VMEM((8, NT), F32),
            pltpu.VMEM((2, TILES, WIDE, WIDE), BF16),
            pltpu.VMEM((2, TILES, WIDE, WIDE), BF16),
            dma((18,)),
            dma((12,)),
            dma((12,)),
            dma((3,)),
            dma((3,)),
            dma((len(SENDS),)),
            dma((len(SENDS),)),
            dma((len(RETURNS),)),
            dma((len(RETURNS),)),
        ],
        compiler_params=pltpu.CompilerParams(collective_id=0, has_side_effects=True, vmem_limit_bytes=VMEM_LIMIT),
    )(
        pinned(mouth_azimuth), pinned(mouth_radius), pinned(mode_impedance), *[pinned(flat(x)) for x in fields], pinned(acoustic), pinned(lam),
        pinned(halves(sines)), pinned(pick), pinned(base), pinned(halves(tiles)), pinned(halves(tiles.transpose(0, 2, 1))),
    )
    results = (dn, press, acn)
    dn, press, acn = pl.pallas_call(
        deliver,
        out_shape=tuple(jax.ShapeDtypeStruct(x.shape, F32) for x in results),
        in_specs=[vmem] * 3,
        out_specs=(anywhere,) * 3,
        scratch_shapes=[dma((3,))],
        compiler_params=pltpu.CompilerParams(vmem_limit_bytes=2**20),
    )(*results)
    return dn.reshape(T, R, NZ), press.reshape(T, R, NZ), acn


def solution(mesh):
    cells, columns = P("sector", "radial", None), P(None, "sector", None)
    return jax.shard_map(
        shards,
        mesh=mesh,
        in_specs=(cells, cells, cells, columns, P(), P(), P()),
        out_specs=(cells, cells, columns),
        check_vma=False,
    )
```
